128 devices in a mesh: tok: 32 (over y, x, core), col: 4 (over z).
Axes of the slice: x: 4, y: 4, z: 4, core: 2. Of those that a mesh axis runs over, the one named last changes fastest.
Arguments:
- samples: bfloat16 [131072, 1024], P('tok', 'col')
- lengths: int32 [32, 16], replicated, may hold values from 1 to 4065, as said below
- sketch: bfloat16 [1024, 1024], replicated
Outputs:
- latent_basis: float32 [1024, 1024], P('tok', 'col')
The draws below stay inside these ranges and needn't reach their ends.
Inputs may be any that keep to these rules, and one draw needn't show every extreme that they name: Each buffer's lengths sum to at most 4096; the sums of buffer i and of the buffer half the tok axis away from it add up to exactly 4096.
All inputs are finite; a program needn't handle non-finite values.
Results may differ from the reference program's by a relative error of at most 0.00037.
Values may be sent and summed in bfloat16 or wider, within the bound.
A program may use at most 128 MiB of HBM per device.

```python
import math
from functools import partial
import jax
import jax.numpy as jnp
from jax import lax

D = 1024
SKETCH = 1024
TOK_DEV = 2048
SEQS = 16
N_TOK = 32


def draw_samples(key, part):
    key = jax.random.fold_in(key, 5)
    key_scale = jax.random.fold_in(key, 1)
    key_value = jax.random.fold_in(key, 2)
    key_factor = jax.random.fold_in(key, 3)
    key_loading = jax.random.fold_in(key, 4)
    total_rows = 2 * TOK_DEV * N_TOK
    factor_count = 8
    scales = jnp.exp(jax.random.uniform(key_scale, (1, D), jnp.float32, math.log(0.5), math.log(2.0)))
    noise = jax.random.normal(key_value, (total_rows, D), jnp.float32)
    near_mix = 0.6
    far_mix = -0.4
    loadings = 0.12 * jax.random.normal(key_loading, (factor_count, D), jnp.float32)
    factors = jax.random.normal(key_factor, (total_rows, factor_count), jnp.float32)
    mixed = noise + near_mix * jnp.roll(noise, 1, axis=1) + far_mix * jnp.roll(noise, 3, axis=1)
    values = mixed * scales
    for index in range(factor_count):
        values = values + factors[:, index:index + 1] * loadings[index][None, :]
    return values.astype(jnp.bfloat16)


def draw_lengths(key, part):
    key = jax.random.fold_in(key, 11)
    capacity = 2 * TOK_DEV
    half_count = N_TOK // 2
    small_live = jax.random.randint(jax.random.fold_in(key, 1), (half_count,), SEQS, capacity // 4 + 1)
    pair_index = lax.iota(jnp.int32, half_count)
    first_half = jnp.where(pair_index % 2 == 1, capacity - small_live, small_live)
    first_half = first_half.at[1].set(capacity - SEQS)
    live_rows = jnp.concatenate([first_half, capacity - first_half]).astype(jnp.int32)
    cut_points = jax.random.randint(jax.random.fold_in(key, 2), (N_TOK, SEQS - 1), 0, 1 << 20)
    cut_points = jnp.sort(cut_points % (live_rows - SEQS + 1)[:, None], axis=1)
    cut_points = cut_points.at[1].set(0)
    lower_edge = jnp.zeros((N_TOK, 1), jnp.int32)
    upper_edge = (live_rows - SEQS)[:, None]
    boundaries = jnp.concatenate([lower_edge, cut_points.astype(jnp.int32), upper_edge], axis=1)
    return (boundaries[:, 1:] - boundaries[:, :-1] + 1).astype(jnp.int32)


def draw_sketch(key, part):
    key = jax.random.fold_in(key, 7)
    key_diag = jax.random.fold_in(key, 1)
    key_spread = jax.random.fold_in(key, 2)
    diag_scale = jnp.exp(jax.random.uniform(key_diag, (SKETCH,), jnp.float32, math.log(0.8), math.log(1.25)))
    spread = jax.random.normal(key_spread, (D, SKETCH), jnp.float32)
    diagonal_mask = lax.iota(jnp.int32, D)[:, None] == lax.iota(jnp.int32, SKETCH)[None, :]
    matrix = jnp.where(diagonal_mask, diag_scale[None, :], jnp.float32(0.0)) + 0.5 * spread / math.sqrt(D)
    return matrix.astype(jnp.bfloat16)


def setup_inputs(seed: int = 0) -> dict:
    key_list = jax.random.split(jax.random.key(seed), 4)
    samples = draw_samples(jax.random.fold_in(key_list[3], 71), 0)
    lengths = draw_lengths(jax.random.fold_in(key_list[3], 71), 0)
    sketch = draw_sketch(jax.random.fold_in(key_list[3], 71), 0)
    return {"samples": samples, "lengths": lengths, "sketch": sketch}


def row_weights(counts, capacity_rows, scale_rows):
    seq_ends = jnp.cumsum(counts)
    seq_starts = seq_ends - counts
    position = lax.iota(jnp.int32, capacity_rows)[None, :]
    covered = (position >= seq_starts[:, None]) & (position < seq_ends[:, None])
    per_sequence = lax.rsqrt(1.0 + 4.0 * counts.astype(jnp.float32) / scale_rows)
    return lax.optimization_barrier(jnp.sum(jnp.where(covered, per_sequence[:, None], jnp.float32(0.0)), axis=0))

def reference(samples, lengths, sketch):
    weighting = partial(row_weights, capacity_rows=2 * TOK_DEV, scale_rows=float(TOK_DEV))
    weights = jax.vmap(weighting)(lengths).reshape(-1)
    sketched = jnp.dot(samples.astype(jnp.float32), sketch.astype(jnp.float32), preferred_element_type=jnp.float32) * weights[:, None]
    gram_matrix = jnp.dot(sketched.T.astype(jnp.float32), sketched.astype(jnp.float32), precision=lax.Precision.HIGHEST, preferred_element_type=jnp.float32)
    lower_factor = jnp.linalg.cholesky(gram_matrix)
    basis = jax.scipy.linalg.solve_triangular(lower_factor, sketched.T, lower=True).astype(jnp.bfloat16)
    projected = jnp.dot(basis.astype(jnp.float32), samples.astype(jnp.float32), preferred_element_type=jnp.float32)
    return projected * math.sqrt(SKETCH / (TOK_DEV * N_TOK))
```

```python
import math
import functools
import jax, jax.numpy as jnp
from jax import lax
from jax.experimental import pallas as pl
from jax.experimental.pallas import tpu as pltpu
from jax.sharding import PartitionSpec as P

F32, BF16 = jnp.float32, jnp.bfloat16
BLK = 128

def split(x):
    hi = x.astype(BF16)
    return hi, (x - hi.astype(F32)).astype(BF16)

def mm_t(a, b):
    return lax.dot_general(a, b, (((1,), (1,)), ((), ())), preferred_element_type=F32)

def mm3_t(a, b):
    (ah, al), (bh, bl) = a, b
    return mm_t(ah, bh) + (mm_t(ah, bl) + mm_t(al, bh))

def inverse_factor(m):
    n = m.shape[0]
    sub = lax.broadcasted_iota(jnp.int32, (8, n), 0)
    t = (lax.broadcasted_iota(jnp.int32, (n, n), 0) == lax.broadcasted_iota(jnp.int32, (n, n), 1)).astype(F32)
    out = []
    for s in range(n // 8):
        ms, ts = m[:8], t[:8]
        m, t = m[8:], t[8:]
        cols = [jnp.broadcast_to(ms[:, 8 * s + k:8 * s + k + 1], (8, n)) for k in range(8)]
        e = [[jnp.broadcast_to(cols[k][i:i + 1], (8, n)) for k in range(i + 1)] for i in range(8)]
        r = []
        for k in range(8):
            r.append(lax.rsqrt(e[k][k]))
            for i in range(k + 1, 8):
                e[i][k] = e[i][k] * r[k]
                for j in range(k + 1, i + 1):
                    e[i][j] = e[i][j] - e[i][k] * e[j][k]
        u, v = [], []
        w = None
        for k in range(8):
            mk = jnp.broadcast_to(ms[k:k + 1], (8, n))
            tk = jnp.broadcast_to(ts[k:k + 1], (8, n))
            for j in range(k):
                mk = mk - e[k][j] * u[j]
                tk = tk - e[k][j] * v[j]
            u.append(mk * r[k])
            v.append(tk * r[k])
            w = v[k] if w is None else jnp.where(sub == k, v[k], w)
        out.append(w)
        rest = m.shape[0] // 8
        ml, tl = [], []
        for q in range(rest):
            mq, tq = m[8 * q:8 * q + 8], t[8 * q:8 * q + 8]
            c = []
            for k in range(8):
                ck = jnp.broadcast_to(mq[:, 8 * s + k:8 * s + k + 1], (8, n))
                for j in range(k):
                    ck = ck - c[j] * e[k][j]
                c.append(ck * r[k])
            for k in range(8):
                mq = mq - c[k] * u[k]
                tq = tq - c[k] * v[k]
            ml.append(mq)
            tl.append(tq)
        if rest:
            m, t = jnp.concatenate(ml, 0), jnp.concatenate(tl, 0)
    return jnp.concatenate(out, 0)

def chol_body(n, extra, e_ref, lh, ll):
    total = n + extra
    nb = n // BLK
    for b in range(nb):
        r0, r1 = b * BLK, (b + 1) * BLK
        w = split(inverse_factor(e_ref[r0:r1, r0:r1]))
        for c in range(b + 1, nb + 1):
            lo, hi = c * BLK, min((c + 1) * BLK, total)
            x = mm3_t(split(e_ref[lo:hi, r0:r1]), w)
            if c == nb:
                e_ref[lo:hi, r0:r1] = x
            xh, xl = split(x)
            lh[lo:hi, :] = xh
            ll[lo:hi, :] = xl
        for c in range(b + 1, nb):
            lo = c * BLK
            e_ref[lo:total, lo:lo + BLK] -= mm3_t((lh[lo:total], ll[lo:total]), (lh[lo:lo + BLK], ll[lo:lo + BLK]))

def kernel(n, extra, g_ref, c_ref, o_ref, e, lh, ll, sem):
    cg = pltpu.make_async_copy(g_ref, e.at[0:n], sem.at[0])
    cc = pltpu.make_async_copy(c_ref, e.at[n:n + extra], sem.at[1])
    cg.start(); cc.start(); cg.wait(); cc.wait()
    chol_body(n, extra, e, lh, ll)
    o_ref[...] = e[n:n + extra, :]

def solve(g, ct):
    n, extra = g.shape[0], ct.shape[0]
    return pl.pallas_call(
        functools.partial(kernel, n, extra),
        out_shape=jax.ShapeDtypeStruct((extra, n), F32),
        in_specs=[pl.BlockSpec(memory_space=pl.ANY)] * 2,
        out_specs=pl.BlockSpec(memory_space=pltpu.VMEM),
        scratch_shapes=[pltpu.VMEM((n + extra, n), F32), pltpu.VMEM((n + extra, BLK), BF16), pltpu.VMEM((n + extra, BLK), BF16), pltpu.SemaphoreType.DMA((2,))],
        compiler_params=pltpu.CompilerParams(vmem_limit_bytes=48 << 20),
        cost_estimate=pl.CostEstimate(flops=2_000_000_000, bytes_accessed=8 << 20, transcendentals=1024),
    )(g, ct)


def row_weights(counts, capacity_rows, scale_rows):
    seq_ends = jnp.cumsum(counts)
    seq_starts = seq_ends - counts
    position = lax.iota(jnp.int32, capacity_rows)[None, :]
    covered = (position >= seq_starts[:, None]) & (position < seq_ends[:, None])
    per_sequence = lax.rsqrt(1.0 + 4.0 * counts.astype(jnp.float32) / scale_rows)
    return jnp.sum(jnp.where(covered, per_sequence[:, None], jnp.float32(0.0)), axis=0)


def halves(x):
    hi = lax.reduce_precision(x, 8, 7)
    return hi.astype(BF16), (x - hi).astype(BF16)


def shards(samples, lengths, sketch):
    rows = samples.shape[0]
    tok, col = lax.axis_size("tok"), lax.axis_size("col")
    me, mc = lax.axis_index("tok"), lax.axis_index("col")
    mine = lax.all_to_all(samples, "col", split_axis=0, concat_axis=1, tiled=True)
    w = row_weights(lax.dynamic_index_in_dim(lengths, me, 0, keepdims=False), rows, float(rows // 2))
    w = lax.dynamic_slice_in_dim(w, mc * (rows // col), rows // col, 0)
    s = jnp.dot(mine, sketch, preferred_element_type=F32) * w[:, None]
    sh, sl = halves(s)
    over = (((0,), (0,)), ((), ()))
    dot = lambda a, b: lax.dot_general(a, b, over, preferred_element_type=F32)
    gram = dot(sh, sh) + (dot(sh, sl) + dot(sl, sh))
    cross = dot(mine, sh) + dot(mine, sl)
    gram = lax.psum(gram, ("tok", "col"))
    cross = lax.psum_scatter(cross, ("col", "tok"), scatter_dimension=0, tiled=True)
    y = solve(gram, jnp.concatenate([cross, jnp.zeros_like(cross)], 0))
    y = y[:cross.shape[0]] * math.sqrt(sketch.shape[1] / (rows // 2 * tok))
    return lax.all_to_all(y, "tok", split_axis=1, concat_axis=0, tiled=True).T


def solution(mesh):
    in_specs = (P("tok", "col"), P(), P())
    out_specs = P("tok", "col")
    return jax.shard_map(shards, mesh=mesh, in_specs=in_specs, out_specs=out_specs, check_vma=False)
```

```python
import functools
import math

import jax
import jax.numpy as jnp
from jax import lax
from jax.experimental import pallas as pl
from jax.experimental.pallas import tpu as pltpu
from jax.sharding import PartitionSpec as P

F32, BF16 = jnp.float32, jnp.bfloat16
MESH = pl.DeviceIdType.MESH

BLK = 128

def split(x):
    hi = x.astype(BF16)
    return hi, (x - hi.astype(F32)).astype(BF16)

def mm_t(a, b):
    return lax.dot_general(a, b, (((1,), (1,)), ((), ())), preferred_element_type=F32)

def mm3_t(a, b):
    (ah, al), (bh, bl) = a, b
    return mm_t(ah, bh) + (mm_t(ah, bl) + mm_t(al, bh))

def inverse_factor(m):
    n = m.shape[0]
    sub = lax.broadcasted_iota(jnp.int32, (8, n), 0)
    t = (lax.broadcasted_iota(jnp.int32, (n, n), 0) == lax.broadcasted_iota(jnp.int32, (n, n), 1)).astype(F32)
    out = []
    for s in range(n // 8):
        ms, ts = m[:8], t[:8]
        m, t = m[8:], t[8:]
        cols = [jnp.broadcast_to(ms[:, 8 * s + k:8 * s + k + 1], (8, n)) for k in range(8)]
        e = [[jnp.broadcast_to(cols[k][i:i + 1], (8, n)) for k in range(i + 1)] for i in range(8)]
        r = []
        for k in range(8):
            r.append(lax.rsqrt(e[k][k]))
            for i in range(k + 1, 8):
                e[i][k] = e[i][k] * r[k]
                for j in range(k + 1, i + 1):
                    e[i][j] = e[i][j] - e[i][k] * e[j][k]
        u, v = [], []
        w = None
        for k in range(8):
            mk = jnp.broadcast_to(ms[k:k + 1], (8, n))
            tk = jnp.broadcast_to(ts[k:k + 1], (8, n))
            for j in range(k):
                mk = mk - e[k][j] * u[j]
                tk = tk - e[k][j] * v[j]
            u.append(mk * r[k])
            v.append(tk * r[k])
            w = v[k] if w is None else jnp.where(sub == k, v[k], w)
        out.append(w)
        rest = m.shape[0] // 8
        ml, tl = [], []
        for q in range(rest):
            mq, tq = m[8 * q:8 * q + 8], t[8 * q:8 * q + 8]
            c = []
            for k in range(8):
                ck = jnp.broadcast_to(mq[:, 8 * s + k:8 * s + k + 1], (8, n))
                for j in range(k):
                    ck = ck - c[j] * e[k][j]
                c.append(ck * r[k])
            for k in range(8):
                mq = mq - c[k] * u[k]
                tq = tq - c[k] * v[k]
            ml.append(mq)
            tl.append(tq)
        if rest:
            m, t = jnp.concatenate(ml, 0), jnp.concatenate(tl, 0)
    return jnp.concatenate(out, 0)

def chol_body(n, extra, e_ref, lh, ll):
    total = n + extra
    nb = n // BLK
    for b in range(nb):
        r0, r1 = b * BLK, (b + 1) * BLK
        w = split(inverse_factor(e_ref[r0:r1, r0:r1]))
        for c in range(b + 1, nb + 1):
            lo, hi = c * BLK, min((c + 1) * BLK, total)
            x = mm3_t(split(e_ref[lo:hi, r0:r1]), w)
            if c == nb:
                e_ref[lo:hi, r0:r1] = x
            xh, xl = split(x)
            lh[lo:hi, :] = xh
            ll[lo:hi, :] = xl
        for c in range(b + 1, nb):
            lo = c * BLK
            e_ref[lo:total, lo:lo + BLK] -= mm3_t((lh[lo:total], ll[lo:total]), (lh[lo:lo + BLK], ll[lo:lo + BLK]))

UNPACK = (
    (0, (0, 256), (0, 256), (0, 0)),
    (0, (256, 512), (0, 512), (256, 0)),
    (0, (256, 512), (512, 640), (512, 0)),
    (1, (256, 512), (0, 640), (512, 128)),
    (0, (0, 256), (256, 640), (768, 0)),
    (1, (0, 256), (0, 640), (768, 384)),
)

def kernel(n, extra, g_ref, c_ref, o_ref, e, lh, ll, sem):
    copies = [pltpu.make_async_copy(c_ref, e.at[n:n + extra], sem.at[6])]
    for i, (h, (r0, r1), (l0, l1), (y, x)) in enumerate(UNPACK):
        copies.append(pltpu.make_async_copy(g_ref.at[h, r0:r1, l0:l1], e.at[y:y + r1 - r0, x:x + l1 - l0], sem.at[i]))
    for c in copies:
        c.start()
    for c in copies:
        c.wait()
    chol_body(n, extra, e, lh, ll)
    o_ref[...] = e[n:n + extra, :]

def solve(g, ct, **kw):
    extra, n = ct.shape
    return pl.pallas_call(
        functools.partial(kernel, n, extra),
        out_shape=jax.ShapeDtypeStruct((extra, n), F32),
        in_specs=[pl.BlockSpec(memory_space=pl.ANY)] * 2,
        out_specs=pl.BlockSpec(memory_space=pltpu.VMEM),
        scratch_shapes=[pltpu.VMEM((n + extra, n), F32), pltpu.VMEM((n + extra, BLK), BF16), pltpu.VMEM((n + extra, BLK), BF16), pltpu.SemaphoreType.DMA((7,))],
        compiler_params=pltpu.CompilerParams(vmem_limit_bytes=48 << 20),
        cost_estimate=pl.CostEstimate(flops=2_000_000_000, bytes_accessed=8 << 20, transcendentals=1024),
        **kw,
    )(g, ct)
G_STREAMS = ((0, 256), (256, 256), (512, 128))
C_STREAMS = ((0, 384), (384, 384), (768, 256))

class Place:
    def __init__(self):
        tok = lax.axis_index("tok")
        self.core = lax.rem(tok, 2)
        self.at = (lax.axis_index("col"), tok // 8, lax.rem(tok // 2, 4))

    def device(self, at, core):
        z, y, x = at
        return ((y * 4 + x) * 2 + core, z)

    def mate(self):
        return self.device(self.at, 1 - self.core)

    def peer(self, axis, d):
        at = list(self.at)
        at[axis] = lax.rem(at[axis] + d, 4)
        return self.device(at, self.core)

    def step(self, axis, d):
        return lax.rem(self.at[axis] + d + 4, 4)

def remote(src, dst, ssem, rsem, dev):
    return pltpu.make_async_remote_copy(src_ref=src, dst_ref=dst, send_sem=ssem, recv_sem=rsem, device_id=dev, device_id_type=MESH)

def pick(axis, p, lanes):
    idx = [slice(None)] * 3
    idx[axis] = p
    return tuple(idx) + (slice(None), pl.ds(*lanes))

def greet(place):
    barrier = pltpu.get_barrier_semaphore()
    pl.semaphore_signal(barrier, inc=1, device_id=place.mate(), device_id_type=MESH)
    for axis in range(3):
        for d in range(1, 4):
            pl.semaphore_signal(barrier, inc=1, device_id=place.peer(axis, d), device_id_type=MESH)
    pl.semaphore_wait(barrier, 10)

class Reduction:
    def __init__(self, place, streams, acc, cin, r1, a1, r2, a2, r3, a3, sems):
        self.place, self.streams = place, streams
        self.acc, self.cin, self.r, self.a = acc, cin, (r1, r2, r3), (a1, a2, a3)
        self.own, self.cs, self.cr, self.ps, self.pr = sems
        self.sends = []

    def load(self, src_own, src_mate):
        pltpu.make_async_copy(src_own, self.acc, self.own.at[0]).start()
        self.src_own = src_own
        self.src_mate = src_mate

    def exchange(self):
        self.core = {}
        for d in (1, 2, 3, 0):
            for s, lanes in enumerate(self.streams):
                slab = pick(s, self.place.step(s, d), lanes)
                c = remote(self.src_mate.at[slab], self.cin.at[slab], self.cs.at[s, d], self.cr.at[s, d], self.place.mate())
                c.start()
                self.core[s, d] = c

    def ready(self):
        pltpu.make_async_copy(self.src_own, self.acc, self.own.at[0]).wait()

    def order(self, s):
        return (s, (s + 1) % 3, (s + 2) % 3)

    def sub(self, s, phase, p):
        if phase == 0:
            return pick(s, p, self.streams[s])
        if phase == 1:
            rest = [a for a in range(3) if a != s]
            return (p,) if rest[0] == self.order(s)[1] else (slice(None), p)
        return (p,)

    def send(self, phase):
        for d in range(1, 4):
            for s in range(3):
                axis = self.order(s)[phase]
                idx = self.sub(s, phase, self.place.step(axis, d))
                src = self.acc if phase == 0 else self.a[phase - 1][s]
                if phase == 0:
                    self.core[s, d].wait_recv()
                    src[idx] = src[idx] + self.cin[idx]
                c = remote(src.at[idx], self.r[phase][s].at[d - 1], self.ps.at[phase, s, d - 1], self.pr.at[phase, s, d - 1], self.place.peer(axis, d))
                c.start()
                self.sends.append(c)
                self.r_wait = getattr(self, "r_wait", {})
                self.r_wait[phase, s, d] = c

    def gather(self, phase):
        for s in range(3):
            axis = self.order(s)[phase]
            idx = self.sub(s, phase, self.place.step(axis, 0))
            src = self.acc if phase == 0 else self.a[phase - 1][s]
            if phase == 0:
                self.core[s, 0].wait_recv()
                total = src[idx] + self.cin[idx]
            else:
                total = src[idx]
            for d in range(1, 4):
                self.r_wait[phase, s, d].wait_recv()
            r = self.r[phase][s]
            self.a[phase][s][...] = (total + r[0]) + (r[1] + r[2])

    def finish(self):
        for c in self.sends:
            c.wait_send()
        for c in self.core.values():
            c.wait_send()

class Spread:
    def __init__(self, red, full, ss, rs, fs, fr):
        self.red, self.full, self.place = red, full, red.place
        self.ss, self.rs, self.fs, self.fr = ss, rs, fs, fr
        self.sends, self.fwd = [], {}

    def region(self, s, fixed, core):
        idx = [slice(None)] * 3
        for axis, p in fixed.items():
            idx[axis] = p
        return self.full.at[(core,) + tuple(idx) + (slice(None), pl.ds(*self.red.streams[s]))]

    def seed(self):
        core, at = self.place.core, self.place.at
        for s in range(3):
            o, n = self.red.streams[s]
            self.full[core, at[0], at[1], at[2], :, o:o + n] = self.red.a[2][s][...]

    def fixed(self, s, phase, d):
        order = self.red.order(s)
        axes = order[:3 - phase]
        f = {a: self.place.at[a] for a in axes}
        f[axes[-1]] = self.place.step(axes[-1], -d)
        return f, axes[-1]

    def send(self, phase):
        for d in range(1, 4):
            for s in range(3):
                f, axis = self.fixed(s, phase, 0)
                reg = self.region(s, f, self.place.core)
                c = remote(reg, reg, self.ss.at[phase, s, d - 1], self.rs.at[phase, s, d - 1], self.place.peer(axis, d))
                c.start()
                self.sends.append(c)

    def arrived(self, phase, s, d):
        f, axis = self.fixed(s, phase, d)
        reg = self.region(s, f, self.place.core)
        remote(reg, reg, self.ss.at[phase, s, d - 1], self.rs.at[phase, s, d - 1], self.place.peer(axis, d)).wait_recv()

    def wait(self, phase):
        for d in range(1, 4):
            for s in range(3):
                self.arrived(phase, s, d)

    def forward(self, s, d):
        f, _ = self.fixed(s, 2, d)
        reg = self.region(s, f, self.place.core)
        c = remote(reg, reg, self.fs.at[s, d], self.fr.at[s, d], self.place.mate())
        c.start()
        self.sends.append(c)

    def finish(self):
        for s in range(3):
            for d in range(4):
                f, _ = self.fixed(s, 2, d)
                reg = self.region(s, f, 1 - self.place.core)
                remote(reg, reg, self.fs.at[s, d], self.fr.at[s, d], self.place.mate()).wait_recv()
        for c in self.sends:
            c.wait_send()

def reduce_scratch(streams):
    lanes = sum(n for _, n in streams)
    def per(shape):
        return [pltpu.VMEM(shape + (8, n), F32) for _, n in streams]
    dma = pltpu.SemaphoreType.DMA
    return [pltpu.VMEM((4, 4, 4, 8, lanes), F32), pltpu.VMEM((4, 4, 4, 8, lanes), F32),
            per((3, 4, 4)), per((4, 4)), per((3, 4)), per((4,)), per((3,)), per(()),
            (dma((1,)), dma((3, 4)), dma((3, 4)), dma((3, 3, 3)), dma((3, 3, 3)))]

def sum_kernel(g_ref, c_ref, go_ref, co_ref, gs, cs, full, ss, rs, fs, fr, osem):
    place = Place()
    core = place.core
    g = Reduction(place, G_STREAMS, *gs)
    c = Reduction(place, C_STREAMS, *cs)
    g.load(g_ref.at[core], g_ref.at[1 - core])
    c.load(c_ref.at[:, core], c_ref.at[:, 1 - core])
    greet(place)
    g.exchange()
    c.exchange()
    g.ready()
    g.send(0)
    c.ready()
    g.gather(0)
    g.send(1)
    c.send(0)
    g.gather(1)
    g.send(2)
    g.gather(2)
    sp = Spread(g, full, ss, rs, fs, fr)
    sp.seed()
    sp.send(0)
    c.gather(0)
    sp.wait(0)
    sp.send(1)
    c.send(1)
    sp.wait(1)
    sp.send(2)
    for s in range(3):
        sp.forward(s, 0)
    c.gather(1)
    c.send(2)
    for d in range(1, 4):
        for s in range(3):
            sp.arrived(2, s, d)
            sp.forward(s, d)
    c.gather(2)
    for s in range(3):
        o, n = C_STREAMS[s]
        co_ref[:, o:o + n] = c.a[2][s][...]
    sp.finish()
    out = pltpu.make_async_copy(full, go_ref, osem.at[0])
    out.start()
    g.finish()
    c.finish()
    out.wait()

def sum_all(g, c):
    dma = pltpu.SemaphoreType.DMA
    return pl.pallas_call(
        sum_kernel,
        out_shape=(jax.ShapeDtypeStruct(g.shape, F32), jax.ShapeDtypeStruct((8, c.shape[-1]), F32)),
        in_specs=[pl.BlockSpec(memory_space=pl.ANY)] * 2,
        out_specs=(pl.BlockSpec(memory_space=pl.ANY), pl.BlockSpec(memory_space=pltpu.VMEM)),
        scratch_shapes=[reduce_scratch(G_STREAMS), reduce_scratch(C_STREAMS), pltpu.VMEM(g.shape, F32),
                        dma((3, 3, 3)), dma((3, 3, 3)), dma((3, 4)), dma((3, 4)), dma((1,))],
        compiler_params=pltpu.CompilerParams(collective_id=1, has_side_effects=True, vmem_limit_bytes=48 << 20),
        cost_estimate=pl.CostEstimate(flops=10_000_000, bytes_accessed=16 << 20, transcendentals=0),
    )(g, c)

def row_weights(counts, capacity_rows, scale_rows):
    seq_ends = jnp.cumsum(counts)
    seq_starts = seq_ends - counts
    position = lax.iota(jnp.int32, capacity_rows)[None, :]
    covered = (position >= seq_starts[:, None]) & (position < seq_ends[:, None])
    per_sequence = lax.rsqrt(1.0 + 4.0 * counts.astype(jnp.float32) / scale_rows)
    return jnp.sum(jnp.where(covered, per_sequence[:, None], jnp.float32(0.0)), axis=0)


def halves(x):
    hi = lax.reduce_precision(x, 8, 7)
    return hi.astype(BF16), (x - hi).astype(BF16)


def shards(samples, lengths, sketch):
    rows = samples.shape[0]
    tok, col = lax.axis_size("tok"), lax.axis_size("col")
    me, mc = lax.axis_index("tok"), lax.axis_index("col")
    mine = lax.all_to_all(samples, "col", split_axis=0, concat_axis=1, tiled=True)
    w = row_weights(lax.dynamic_index_in_dim(lengths, me, 0, keepdims=False), rows, float(rows // 2))
    w = lax.dynamic_slice_in_dim(w, mc * (rows // col), rows // col, 0)
    s = jnp.dot(mine, sketch, preferred_element_type=F32) * w[:, None]
    sh, sl = halves(s)
    over = (((0,), (0,)), ((), ()))
    dot = lambda a, b: lax.dot_general(a, b, over, preferred_element_type=F32)
    gram = dot(sh, sh) + (dot(sh, sl) + dot(sl, sh))
    cross = dot(mine, sh) + dot(mine, sl)
    packed = jnp.concatenate([
        jnp.concatenate([gram[0:256, 0:256], gram[768:1024]], 1),
        jnp.concatenate([gram[256:512, 0:512], gram[512:768, 0:768]], 1),
    ], 0)
    packed = jnp.stack([packed[:, :640], packed[:, 640:]]).reshape(2, 4, 4, 4, 8, 640)
    total, mine_c = sum_all(packed, cross.reshape(4, 2, 4, 4, 8, 1024))
    y = solve(total.reshape(2, 512, 640), jnp.concatenate([mine_c, jnp.zeros_like(mine_c)], 0))
    y = y[:8] * math.sqrt(sketch.shape[1] / (rows // 2 * tok))
    got = lax.all_to_all(y, "tok", split_axis=1, concat_axis=0, tiled=True)
    got = got.reshape(16, 2, 8, 32).transpose(3, 1, 0, 2)
    return got.reshape(32, 256)


def solution(mesh):
    in_specs = (P("tok", "col"), P(), P())
    out_specs = P("tok", "col")
    return jax.shard_map(shards, mesh=mesh, in_specs=in_specs, out_specs=out_specs, check_vma=False)
```

```python
import functools
import math

import jax
import jax.numpy as jnp
from jax import lax
from jax.experimental import pallas as pl
from jax.experimental.pallas import tpu as pltpu
from jax.sharding import PartitionSpec as P

F32, BF16 = jnp.float32, jnp.bfloat16
MESH = pl.DeviceIdType.MESH
G_STREAMS = ((0, 256), (256, 256), (512, 128))
C_STREAMS = ((0, 384), (384, 384), (768, 256))
G_PLACES = ((0, 512), (1, 384), (1, 0), (0, 0))
SUBS = 4

class Place:
    def __init__(self):
        self.tok = lax.axis_index("tok")
        self.core = lax.rem(self.tok, 2)
        self.at = (lax.axis_index("col"), self.tok // 8, lax.rem(self.tok // 2, 4))

    def device(self, at, core):
        z, y, x = at
        return ((y * 4 + x) * 2 + core, z)

    def mate(self):
        return self.device(self.at, 1 - self.core)

    def peer(self, axis, d):
        at = list(self.at)
        at[axis] = lax.rem(at[axis] + d, 4)
        return self.device(at, self.core)

    def step(self, axis, d):
        return lax.rem(self.at[axis] + d + 4, 4)

def remote(src, dst, ssem, rsem, dev):
    return pltpu.make_async_remote_copy(src_ref=src, dst_ref=dst, send_sem=ssem, recv_sem=rsem, device_id=dev, device_id_type=MESH)

def pick(axis, p, lanes):
    idx = [slice(None)] * 3
    idx[axis] = p
    return tuple(idx) + (slice(None), pl.ds(*lanes))

def greet(place):
    barrier = pltpu.get_barrier_semaphore()
    pl.semaphore_signal(barrier, inc=1, device_id=place.mate(), device_id_type=MESH)
    for axis in range(3):
        for d in range(1, 4):
            pl.semaphore_signal(barrier, inc=1, device_id=place.peer(axis, d), device_id_type=MESH)
    pl.semaphore_wait(barrier, 10)

class Reduction:
    def __init__(self, place, streams, acc, r1, a1, r2, a2, r3, a3, ps, pr):
        self.place, self.streams = place, streams
        self.acc, self.r, self.a = acc, (r1, r2, r3), (a1, a2, a3)
        self.ps, self.pr = ps, pr
        self.copies = {}

    def order(self, s):
        return (s, (s + 1) % 3, (s + 2) % 3)

    def sub(self, s, phase, p):
        if phase == 0:
            return pick(s, p, self.streams[s])
        if phase == 1 and s == 1:
            return (slice(None), p)
        return (p,)

    def source(self, s, phase):
        return self.acc if phase == 0 else self.a[phase - 1][s]

    def send(self, phase, s):
        axis = self.order(s)[phase]
        for d in (2, 1, 3):
            src = self.source(s, phase).at[self.sub(s, phase, self.place.step(axis, d))]
            c = remote(src, self.r[phase][s].at[d - 1], self.ps.at[phase, s, d - 1], self.pr.at[phase, s, d - 1], self.place.peer(axis, d))
            c.start()
            self.copies[phase, s, d] = c

    def gather(self, phase, s):
        axis = self.order(s)[phase]
        total = self.source(s, phase)[self.sub(s, phase, self.place.step(axis, 0))]
        for d in range(1, 4):
            self.copies[phase, s, d].wait_recv()
        r = self.r[phase][s]
        self.a[phase][s][...] = (total + r[0]) + (r[1] + r[2])

    def finish(self):
        for c in self.copies.values():
            c.wait_send()

class Spread:
    def __init__(self, red, full, ss, rs, fs, fr):
        self.red, self.full, self.place = red, full, red.place
        self.ss, self.rs, self.fs, self.fr = ss, rs, fs, fr
        self.sends = []

    def region(self, s, fixed, core):
        idx = [slice(None)] * 3
        for axis, p in fixed.items():
            idx[axis] = p
        return self.full.at[(core,) + tuple(idx) + (slice(None), pl.ds(*self.red.streams[s]))]

    def seed(self, s):
        core, at = self.place.core, self.place.at
        o, n = self.red.streams[s]
        self.full[core, at[0], at[1], at[2], :, o:o + n] = self.red.a[2][s][...]

    def fixed(self, s, phase, d):
        axes = self.red.order(s)[:3 - phase]
        f = {a: self.place.at[a] for a in axes}
        f[axes[-1]] = self.place.step(axes[-1], -d)
        return f, axes[-1]

    def copy(self, phase, s, d, held):
        f, axis = self.fixed(s, phase, held)
        reg = self.region(s, f, self.place.core)
        return remote(reg, reg, self.ss.at[phase, s, d - 1], self.rs.at[phase, s, d - 1], self.place.peer(axis, d))

    def send(self, phase, s):
        for d in (2, 1, 3):
            c = self.copy(phase, s, d, 0)
            c.start()
            self.sends.append(c)

    def arrived(self, phase, s, d):
        self.copy(phase, s, d, d).wait_recv()

    def wait(self, phase, s):
        for d in range(1, 4):
            self.arrived(phase, s, d)

    def passing(self, s, d, core):
        f, _ = self.fixed(s, 2, d)
        reg = self.region(s, f, core)
        return remote(reg, reg, self.fs.at[s, d], self.fr.at[s, d], self.place.mate())

    def forward(self, s, d):
        c = self.passing(s, d, self.place.core)
        c.start()
        self.sends.append(c)

    def finish(self):
        for s in range(3):
            for d in range(4):
                self.passing(s, d, 1 - self.place.core).wait_recv()
        for c in self.sends:
            c.wait_send()

class Rows:
    def __init__(self, place, x, held, loc, zs, zr, ms, mr):
        self.place, self.x, self.held = place, x, held
        self.loc, self.zs, self.zr, self.ms, self.mr = loc, zs, zr, ms, mr
        self.step = held.shape[2] // SUBS

    def rows(self, sub):
        return pl.ds(sub * self.step, self.step)

    def slot(self, core, d, sub):
        return self.held.at[core, self.place.step(0, -d), self.rows(sub)]

    def own(self, sub):
        return pltpu.make_async_copy(self.x.at[self.place.at[0], self.rows(sub)], self.slot(self.place.core, 0, sub), self.loc.at[sub])

    def across(self, d, sub):
        return remote(self.x.at[self.place.step(0, d), self.rows(sub)], self.slot(self.place.core, 0, sub),
                      self.zs.at[sub, d - 1], self.zr.at[sub, d - 1], self.place.peer(0, d))

    def passing(self, d, sub, core):
        src = self.x.at[self.place.at[0], self.rows(sub)] if d == 0 else self.slot(core, d, sub)
        return remote(src, self.slot(core, d, sub), self.ms.at[sub, d], self.mr.at[sub, d], self.place.mate())

    def take(self, sub):
        self.own(sub).wait()
        for d in (1, 3, 2):
            remote(self.slot(self.place.core, d, sub), self.slot(self.place.core, d, sub),
                   self.zs.at[sub, d - 1], self.zr.at[sub, d - 1], self.place.peer(0, d)).wait_recv()
            self.passing(d, sub, self.place.core).start()

    def take_other(self, sub):
        for d in range(4):
            self.passing(d, sub, 1 - self.place.core).wait_recv()

    def finish(self):
        for sub in range(SUBS):
            for d in range(4):
                self.passing(d, sub, self.place.core).wait_send()
                if d:
                    self.across(d, sub).wait_send()

def over_rows(a, b):
    return lax.dot_general(a, b, (((0,), (0,)), ((), ())), preferred_element_type=F32)

def weights_into(place, lengths, wcol):
    rows = wcol.shape[1]
    assert rows == 1024
    pos = place.at[0] * rows + lax.broadcasted_iota(jnp.int32, (8, 128), 0) * 128 + lax.broadcasted_iota(jnp.int32, (8, 128), 1)
    for k in range(2):
        buf = place.tok - place.core + k
        start = jnp.zeros((8, 128), jnp.int32)
        w = jnp.zeros((8, 128), F32)
        for s in range(lengths.shape[1]):
            count = jnp.full((8, 128), lengths[buf, s], jnp.int32)
            per = lax.rsqrt(1.0 + 4.0 * count.astype(F32) / float(2 * rows))
            w = w + jnp.where((pos >= start) & (pos < start + count), per, 0.0)
            start = start + count
        wt = w.T
        for a in range(8):
            wcol[k, 128 * a:128 * (a + 1)] = jnp.broadcast_to(wt[:, a:a + 1], (128, 128))

def front_kernel(len_ref, x_ref, sk_ref, go_ref, co_ref, held, omega, wcol, sh, sl, gs, cs, full, ss, rs, fs, fr, loc, zs, zr, ms, mr, osem):
    place = Place()
    core = place.core
    rows = Rows(place, x_ref, held, loc, zs, zr, ms, mr)
    g = Reduction(place, G_STREAMS, *gs)
    c = Reduction(place, C_STREAMS, *cs)
    sketch = pltpu.make_async_copy(sk_ref, omega, osem.at[0])
    sketch.start()
    for sub in range(SUBS):
        rows.own(sub).start()
    greet(place)
    for sub in range(SUBS):
        for d in (2, 1, 3):
            rows.across(d, sub).start()
        rows.passing(0, sub, core).start()
    weights_into(place, len_ref, wcol)
    g.acc[...] = jnp.zeros_like(g.acc)
    c.acc[...] = jnp.zeros_like(c.acc)
    sketch.wait()
    step = rows.step

    def project(sub, k, which):
        prod = jnp.zeros((step, omega.shape[1]), F32)
        for z in range(4):
            prod += jnp.dot(held[which, z, pl.ds(sub * step, step)], omega[256 * z:256 * (z + 1)], preferred_element_type=F32)
        w = wcol[which, pl.ds(sub * step, step)]
        s = prod * jnp.concatenate([w] * (omega.shape[1] // 128), 1)
        hi = s.astype(BF16)
        at = pl.ds((2 * sub + k) * step, step)
        sh[at] = hi
        sl[at] = (s - hi.astype(F32)).astype(BF16)

    def chunk(sub, _):
        rows.take(sub)
        project(sub, 0, core)
        rows.take_other(sub)
        project(sub, 1, 1 - core)
        at = pl.ds(2 * sub * step, 2 * step)
        for i in range(4):
            width = 128 * (i + 1)
            far = pl.ds(pl.multiple_of(core * width, 128), width)
            lh, ll, rh, rl = sh[at, 256 * i:256 * (i + 1)], sl[at, 256 * i:256 * (i + 1)], sh[at, far], sl[at, far]
            v = over_rows(lh, rh) + over_rows(lh, rl) + over_rows(ll, rh)
            half, lane = G_PLACES[i]
            g.acc[2 * half:2 * half + 2, :, :, :, lane:lane + width] += v.reshape(2, 4, 4, 8, width)
        return 0

    lax.fori_loop(0, SUBS, chunk, 0)
    for s in range(3):
        g.send(0, s)

    def cross(sub, _):
        mine = pl.ds(pl.multiple_of(core * 128, 128), 128)
        for k in range(2):
            which = core if k == 0 else 1 - core
            x = jnp.concatenate([held[which, z, pl.ds(sub * step, step), mine] for z in range(4)], 1)
            at = pl.ds((2 * sub + k) * step, step)
            v = over_rows(x, sh[at]) + over_rows(x, sl[at])
            c.acc[...] += v.reshape(4, 4, 4, 8, omega.shape[1])
        return 0

    lax.fori_loop(0, SUBS, cross, 0)
    sp = Spread(g, full, ss, rs, fs, fr)
    for s in range(3):
        g.gather(0, s)
        g.send(1, s)
    for s in range(3):
        c.send(0, s)
    for s in range(3):
        g.gather(1, s)
        g.send(2, s)
    for s in range(3):
        g.gather(2, s)
        sp.seed(s)
        sp.send(0, s)
    for s in range(3):
        sp.wait(0, s)
        sp.send(1, s)
    for s in range(3):
        c.gather(0, s)
        c.send(1, s)
    for s in range(3):
        sp.wait(1, s)
        sp.send(2, s)
        sp.forward(s, 0)
    for s in range(3):
        c.gather(1, s)
        c.send(2, s)
    for d in (1, 3, 2):
        for s in range(3):
            sp.arrived(2, s, d)
            sp.forward(s, d)
    for s in range(3):
        c.gather(2, s)
        o, n = C_STREAMS[s]
        co_ref[0:8, o:o + n] = c.a[2][s][...]
    co_ref[8:16, :] = jnp.zeros((8, omega.shape[1]), F32)
    sp.finish()
    out = pltpu.make_async_copy(full, go_ref, osem.at[0])
    out.start()
    rows.finish()
    g.finish()
    c.finish()
    out.wait()

def reduce_scratch(streams):
    lanes = sum(n for _, n in streams)
    def per(shape):
        return [pltpu.VMEM(shape + (8, n), F32) for _, n in streams]
    dma = pltpu.SemaphoreType.DMA
    return [pltpu.VMEM((4, 4, 4, 8, lanes), F32), per((3, 4, 4)), per((4, 4)), per((3, 4)), per((4,)), per((3,)), per(()),
            dma((3, 3, 3)), dma((3, 3, 3))]

def front(lengths, samples, sketch):
    dma = pltpu.SemaphoreType.DMA
    rows, feats = samples.shape
    width = sketch.shape[1]
    chunk = rows // 4
    return pl.pallas_call(
        front_kernel,
        out_shape=(jax.ShapeDtypeStruct((2, 4, 4, 4, 8, 640), F32), jax.ShapeDtypeStruct((16, width), F32)),
        in_specs=[pl.BlockSpec(memory_space=pltpu.SMEM), pl.BlockSpec(memory_space=pl.ANY), pl.BlockSpec(memory_space=pl.ANY)],
        out_specs=(pl.BlockSpec(memory_space=pl.ANY), pl.BlockSpec(memory_space=pltpu.VMEM)),
        scratch_shapes=[pltpu.VMEM((2, 4, chunk, feats), BF16), pltpu.VMEM(sketch.shape, BF16), pltpu.VMEM((2, chunk, 128), F32),
                        pltpu.VMEM((2 * chunk, width), BF16), pltpu.VMEM((2 * chunk, width), BF16),
                        reduce_scratch(G_STREAMS), reduce_scratch(C_STREAMS), pltpu.VMEM((2, 4, 4, 4, 8, 640), F32),
                        dma((3, 3, 3)), dma((3, 3, 3)), dma((3, 4)), dma((3, 4)),
                        dma((SUBS,)), dma((SUBS, 3)), dma((SUBS, 3)), dma((SUBS, 4)), dma((SUBS, 4)), dma((1,))],
        compiler_params=pltpu.CompilerParams(collective_id=1, has_side_effects=True, vmem_limit_bytes=56 << 20),
        cost_estimate=pl.CostEstimate(flops=13_000_000_000, bytes_accessed=8 << 20, transcendentals=0),
    )(lengths, samples.reshape(4, chunk, feats), sketch)

def swap_kernel(scale, y_ref, o_ref, got, flat, ssem, rsem):
    place = Place()
    tok = place.tok
    barrier = pltpu.get_barrier_semaphore()
    count = 32
    def hello(d, _):
        pl.semaphore_signal(barrier, inc=1, device_id=(lax.rem(tok + d, count), place.at[0]), device_id_type=MESH)
        return 0
    lax.fori_loop(1, count, hello, 0)
    pl.semaphore_wait(barrier, count - 1)
    def copy(d, owner):
        to = lax.rem(tok + d, count)
        lanes = pl.ds(pl.multiple_of((to // 4) * 128, 128), 128)
        return remote(y_ref.at[0:8, lanes], got.at[lax.rem(owner, 2), owner // 2], ssem.at[d], rsem.at[d], (to, place.at[0]))
    def start(d, _):
        copy(d, tok).start()
        return 0
    lax.fori_loop(1, count, start, 0)
    got[place.core, tok // 2] = y_ref[0:8, pl.ds(pl.multiple_of((tok // 4) * 128, 128), 128)]
    def done(d, _):
        copy(d, lax.rem(tok + count - d, count)).wait_recv()
        return 0
    lax.fori_loop(1, count, done, 0)
    for k in range(2):
        flat[:, 128 * k:128 * (k + 1)] = got[k].reshape(128, 128).T * scale
    o_ref[...] = flat[pl.ds(pl.multiple_of(lax.rem(tok, 4) * 32, 32), 32)]
    def sent(d, _):
        copy(d, tok).wait_send()
        return 0
    lax.fori_loop(1, count, sent, 0)

def swap(y, scale):
    dma = pltpu.SemaphoreType.DMA
    return pl.pallas_call(
        functools.partial(swap_kernel, scale),
        out_shape=jax.ShapeDtypeStruct((32, 256), F32),
        in_specs=[pl.BlockSpec(memory_space=pltpu.VMEM)],
        out_specs=pl.BlockSpec(memory_space=pltpu.VMEM),
        scratch_shapes=[pltpu.VMEM((2, 16, 8, 128), F32), pltpu.VMEM((128, 256), F32), dma((32,)), dma((32,))],
        compiler_params=pltpu.CompilerParams(collective_id=2, has_side_effects=True),
        cost_estimate=pl.CostEstimate(flops=0, bytes_accessed=1 << 20, transcendentals=0),
    )(y)

BLK = 128

def split(x):
    hi = x.astype(BF16)
    return hi, (x - hi.astype(F32)).astype(BF16)

def mm_t(a, b):
    return lax.dot_general(a, b, (((1,), (1,)), ((), ())), preferred_element_type=F32)

def mm3_t(a, b):
    (ah, al), (bh, bl) = a, b
    return mm_t(ah, bh) + (mm_t(ah, bl) + mm_t(al, bh))

def inverse_factor(m):
    n = m.shape[0]
    sub = lax.broadcasted_iota(jnp.int32, (8, n), 0)
    t = (lax.broadcasted_iota(jnp.int32, (n, n), 0) == lax.broadcasted_iota(jnp.int32, (n, n), 1)).astype(F32)
    out = []
    for s in range(n // 8):
        ms, ts = m[:8], t[:8]
        m, t = m[8:], t[8:]
        cols = [jnp.broadcast_to(ms[:, 8 * s + k:8 * s + k + 1], (8, n)) for k in range(8)]
        e = [[jnp.broadcast_to(cols[k][i:i + 1], (8, n)) for k in range(i + 1)] for i in range(8)]
        r = []
        for k in range(8):
            r.append(lax.rsqrt(e[k][k]))
            for i in range(k + 1, 8):
                e[i][k] = e[i][k] * r[k]
                for j in range(k + 1, i + 1):
                    e[i][j] = e[i][j] - e[i][k] * e[j][k]
        u, v = [], []
        w = None
        for k in range(8):
            mk = jnp.broadcast_to(ms[k:k + 1], (8, n))
            tk = jnp.broadcast_to(ts[k:k + 1], (8, n))
            for j in range(k):
                mk = mk - e[k][j] * u[j]
                tk = tk - e[k][j] * v[j]
            u.append(mk * r[k])
            v.append(tk * r[k])
            w = v[k] if w is None else jnp.where(sub == k, v[k], w)
        out.append(w)
        rest = m.shape[0] // 8
        ml, tl = [], []
        for q in range(rest):
            mq, tq = m[8 * q:8 * q + 8], t[8 * q:8 * q + 8]
            c = []
            for k in range(8):
                ck = jnp.broadcast_to(mq[:, 8 * s + k:8 * s + k + 1], (8, n))
                for j in range(k):
                    ck = ck - c[j] * e[k][j]
                c.append(ck * r[k])
            for k in range(8):
                mq = mq - c[k] * u[k]
                tq = tq - c[k] * v[k]
            ml.append(mq)
            tl.append(tq)
        if rest:
            m, t = jnp.concatenate(ml, 0), jnp.concatenate(tl, 0)
    return jnp.concatenate(out, 0)

def chol_body(n, extra, e_ref, lh, ll):
    total = n + extra
    nb = n // BLK
    for b in range(nb):
        r0, r1 = b * BLK, (b + 1) * BLK
        w = split(inverse_factor(e_ref[r0:r1, r0:r1]))
        for c in range(b + 1, nb + 1):
            lo, hi = c * BLK, min((c + 1) * BLK, total)
            x = mm3_t(split(e_ref[lo:hi, r0:r1]), w)
            if c == nb:
                e_ref[lo:hi, r0:r1] = x
            xh, xl = split(x)
            lh[lo:hi, :] = xh
            ll[lo:hi, :] = xl
        for c in range(b + 1, nb):
            lo = c * BLK
            e_ref[lo:total, lo:lo + BLK] -= mm3_t((lh[lo:total], ll[lo:total]), (lh[lo:lo + BLK], ll[lo:lo + BLK]))

def unpack(g_ref, e, sem):
    copies = []
    for i, (half, lane) in enumerate(G_PLACES):
        width = 128 * (i + 1)
        for core in range(2):
            src = g_ref.at[core, 256 * half:256 * (half + 1), lane:lane + width]
            copies.append(pltpu.make_async_copy(src, e.at[256 * i:256 * (i + 1), core * width:(core + 1) * width], sem.at[2 * i + core]))
    return copies

def kernel(n, extra, g_ref, c_ref, o_ref, e, lh, ll, sem):
    copies = [pltpu.make_async_copy(c_ref, e.at[n:n + extra], sem.at[8])] + unpack(g_ref, e, sem)
    for c in copies:
        c.start()
    for c in copies:
        c.wait()
    chol_body(n, extra, e, lh, ll)
    o_ref[...] = e[n:n + extra, :]

def solve(g, ct, **kw):
    extra, n = ct.shape
    return pl.pallas_call(
        functools.partial(kernel, n, extra),
        out_shape=jax.ShapeDtypeStruct((extra, n), F32),
        in_specs=[pl.BlockSpec(memory_space=pl.ANY)] * 2,
        out_specs=pl.BlockSpec(memory_space=pltpu.VMEM),
        scratch_shapes=[pltpu.VMEM((n + extra, n), F32), pltpu.VMEM((n + extra, BLK), BF16), pltpu.VMEM((n + extra, BLK), BF16), pltpu.SemaphoreType.DMA((9,))],
        compiler_params=pltpu.CompilerParams(vmem_limit_bytes=48 << 20),
        cost_estimate=pl.CostEstimate(flops=2_000_000_000, bytes_accessed=8 << 20, transcendentals=1024),
        **kw,
    )(g, ct)


def shards(samples, lengths, sketch):
    total, mine = front(lengths, samples, sketch)
    y = solve(total.reshape(2, 512, 640), mine)
    scale = math.sqrt(sketch.shape[1] / (samples.shape[0] // 2 * lax.axis_size("tok")))
    return swap(y, scale)


def solution(mesh):
    in_specs = (P("tok", "col"), P(), P())
    out_specs = P("tok", "col")
    return jax.shard_map(shards, mesh=mesh, in_specs=in_specs, out_specs=out_specs, check_vma=False)
```

```python
import functools
import math

import jax
import jax.numpy as jnp
from jax import lax
from jax.experimental import pallas as pl
from jax.experimental.pallas import tpu as pltpu
from jax.sharding import PartitionSpec as P

F32, BF16 = jnp.float32, jnp.bfloat16
MESH = pl.DeviceIdType.MESH
G_STREAMS = ((0, 256), (256, 256), (512, 128))
C_STREAMS = ((0, 256), (256, 384), (640, 384))
G_PLACES = ((0, 512), (1, 384), (1, 0), (0, 0))
SUBS = 4

class Place:
    def __init__(self):
        self.tok = lax.axis_index("tok")
        self.core = lax.rem(self.tok, 2)
        self.at = (lax.axis_index("col"), self.tok // 8, lax.rem(self.tok // 2, 4))

    def device(self, at, core):
        z, y, x = at
        return ((y * 4 + x) * 2 + core, z)

    def mate(self):
        return self.device(self.at, 1 - self.core)

    def peer(self, axis, d):
        at = list(self.at)
        at[axis] = lax.rem(at[axis] + d, 4)
        return self.device(at, self.core)

    def step(self, axis, d):
        return lax.rem(self.at[axis] + d + 4, 4)

def remote(src, dst, ssem, rsem, dev):
    return pltpu.make_async_remote_copy(src_ref=src, dst_ref=dst, send_sem=ssem, recv_sem=rsem, device_id=dev, device_id_type=MESH)

def pick(axis, p, lanes):
    idx = [slice(None)] * 3
    idx[axis] = p
    return tuple(idx) + (slice(None), pl.ds(*lanes))

def greet(place):
    barrier = pltpu.get_barrier_semaphore()
    pl.semaphore_signal(barrier, inc=1, device_id=place.mate(), device_id_type=MESH)
    for axis in range(3):
        for d in range(1, 4):
            pl.semaphore_signal(barrier, inc=1, device_id=place.peer(axis, d), device_id_type=MESH)
    pl.semaphore_wait(barrier, 10)

class Reduction:
    def __init__(self, place, streams, acc, r1, a1, r2, a2, r3, a3, ps, pr):
        self.place, self.streams = place, streams
        self.acc, self.r, self.a = acc, (r1, r2, r3), (a1, a2, a3)
        self.ps, self.pr = ps, pr
        self.copies = {}

    def order(self, s):
        return (s, (s + 1) % 3, (s + 2) % 3)

    def sub(self, s, phase, p):
        if phase == 0:
            return pick(s, p, self.streams[s])
        if phase == 1 and s == 1:
            return (slice(None), p)
        return (p,)

    def source(self, s, phase):
        return self.acc if phase == 0 else self.a[phase - 1][s]

    def send(self, phase, s):
        axis = self.order(s)[phase]
        for d in (2, 1, 3):
            src = self.source(s, phase).at[self.sub(s, phase, self.place.step(axis, d))]
            c = remote(src, self.r[phase][s].at[d - 1], self.ps.at[phase, s, d - 1], self.pr.at[phase, s, d - 1], self.place.peer(axis, d))
            c.start()
            self.copies[phase, s, d] = c

    def gather(self, phase, s):
        axis = self.order(s)[phase]
        total = self.source(s, phase)[self.sub(s, phase, self.place.step(axis, 0))]
        for d in range(1, 4):
            self.copies[phase, s, d].wait_recv()
        r = self.r[phase][s]
        self.a[phase][s][...] = (total + r[0]) + (r[1] + r[2])

    def share(self, s):
        axis = self.order(s)[2]
        for d in (2, 1, 3):
            c = remote(self.a[1][s], self.r[2][s].at[d - 1], self.ps.at[2, s, d - 1], self.pr.at[2, s, d - 1], self.place.peer(axis, d))
            c.start()
            self.copies[2, s, d] = c

    def shared(self, s):
        for d in range(1, 4):
            self.copies[2, s, d].wait_recv()
        r = self.r[2][s]
        return (self.a[1][s][...] + r[0]) + (r[1] + r[2])

    def finish(self):
        for c in self.copies.values():
            c.wait_send()

class Spread:
    def __init__(self, red, full, out, ss, rs, fs, fr, ws):
        self.red, self.full, self.place = red, full, red.place
        self.ss, self.rs, self.fs, self.fr, self.ws = ss, rs, fs, fr, ws
        self.out = out
        self.sends, self.writes = [], []

    def region(self, s, fixed, core):
        idx = [slice(None)] * 3
        for axis, p in fixed.items():
            idx[axis] = p
        return self.full.at[(core,) + tuple(idx) + (slice(None), pl.ds(*self.red.streams[s]))]

    def seed(self, s):
        idx = [slice(None)] * 3
        for axis in self.red.order(s)[:2]:
            idx[axis] = self.place.at[axis]
        o, n = self.red.streams[s]
        self.full[(self.place.core,) + tuple(idx) + (slice(None), slice(o, o + n))] = self.red.shared(s)

    def fixed(self, s, phase, d):
        axes = self.red.order(s)[:3 - phase]
        f = {a: self.place.at[a] for a in axes}
        f[axes[-1]] = self.place.step(axes[-1], -d)
        return f, axes[-1]

    def copy(self, phase, s, d, held):
        f, axis = self.fixed(s, phase, held)
        reg = self.region(s, f, self.place.core)
        return remote(reg, reg, self.ss.at[phase, s, d - 1], self.rs.at[phase, s, d - 1], self.place.peer(axis, d))

    def send(self, phase, s):
        for d in (2, 1, 3):
            c = self.copy(phase, s, d, 0)
            c.start()
            self.sends.append(c)

    def arrived(self, phase, s, d):
        self.copy(phase, s, d, d).wait_recv()

    def wait(self, phase, s):
        for d in range(1, 4):
            self.arrived(phase, s, d)

    def passing(self, s, d, core):
        f, _ = self.fixed(s, 2, d)
        reg = self.region(s, f, core)
        return remote(reg, reg, self.fs.at[s, d], self.fr.at[s, d], self.place.mate())

    def write(self, s, d, core):
        f, _ = self.fixed(s, 2, d)
        idx = [slice(None)] * 3
        for axis, p in f.items():
            idx[axis] = p
        idx = (core,) + tuple(idx) + (slice(None), pl.ds(*self.red.streams[s]))
        c = pltpu.make_async_copy(self.full.at[idx], self.out.at[idx], self.ws.at[s, d, 0 if core is self.place.core else 1])
        c.start()
        self.writes.append(c)

    def forward(self, s, d):
        c = self.passing(s, d, self.place.core)
        c.start()
        self.sends.append(c)
        self.write(s, d, self.place.core)

    def finish(self):
        for d in (0, 1, 3, 2):
            for s in range(3):
                self.passing(s, d, 1 - self.place.core).wait_recv()
                self.write(s, d, 1 - self.place.core)
        for c in self.sends:
            c.wait_send()
        for c in self.writes:
            c.wait()

class Rows:
    def __init__(self, place, x, held, loc, zs, zr, ms, mr):
        self.place, self.x, self.held = place, x, held
        self.loc, self.zs, self.zr, self.ms, self.mr = loc, zs, zr, ms, mr
        self.step = held.shape[2] // SUBS

    def rows(self, sub):
        return pl.ds(sub * self.step, self.step)

    def slot(self, core, d, sub):
        return self.held.at[core, self.place.step(0, -d), self.rows(sub)]

    def own(self, sub):
        return pltpu.make_async_copy(self.x.at[self.place.at[0], self.rows(sub)], self.slot(self.place.core, 0, sub), self.loc.at[sub])

    def across(self, d, sub):
        return remote(self.x.at[self.place.step(0, d), self.rows(sub)], self.slot(self.place.core, 0, sub),
                      self.zs.at[sub, d - 1], self.zr.at[sub, d - 1], self.place.peer(0, d))

    def passing(self, d, sub, core):
        src = self.x.at[self.place.at[0], self.rows(sub)] if d == 0 else self.slot(core, d, sub)
        return remote(src, self.slot(core, d, sub), self.ms.at[sub, d], self.mr.at[sub, d], self.place.mate())

    def take(self, sub):
        self.own(sub).wait()
        for d in (1, 3, 2):
            remote(self.slot(self.place.core, d, sub), self.slot(self.place.core, d, sub),
                   self.zs.at[sub, d - 1], self.zr.at[sub, d - 1], self.place.peer(0, d)).wait_recv()
            self.passing(d, sub, self.place.core).start()

    def take_other(self, sub):
        for d in range(4):
            self.passing(d, sub, 1 - self.place.core).wait_recv()

    def finish(self):
        for sub in range(SUBS):
            for d in range(4):
                self.passing(d, sub, self.place.core).wait_send()
                if d:
                    self.across(d, sub).wait_send()

def over_rows(a, b):
    return lax.dot_general(a, b, (((0,), (0,)), ((), ())), preferred_element_type=F32)

def weights_into(place, lengths, wcol):
    rows = wcol.shape[1]
    assert rows == 1024
    pos = place.at[0] * rows + lax.broadcasted_iota(jnp.int32, (8, 128), 0) * 128 + lax.broadcasted_iota(jnp.int32, (8, 128), 1)
    for k in range(2):
        buf = place.tok - place.core + k
        start = jnp.zeros((8, 128), jnp.int32)
        w = jnp.zeros((8, 128), F32)
        for s in range(lengths.shape[1]):
            count = jnp.full((8, 128), lengths[buf, s], jnp.int32)
            per = lax.rsqrt(1.0 + 4.0 * count.astype(F32) / float(2 * rows))
            w = w + jnp.where((pos >= start) & (pos < start + count), per, 0.0)
            start = start + count
        wt = w.T
        for a in range(8):
            wcol[k, 128 * a:128 * (a + 1)] = jnp.broadcast_to(wt[:, a:a + 1], (128, 128))

def front_kernel(len_ref, x_ref, sk_ref, go_ref, co_ref, held, omega, wcol, sh, sl, gs, cs, full, ss, rs, fs, fr, ws, loc, zs, zr, ms, mr, osem):
    place = Place()
    core = place.core
    rows = Rows(place, x_ref, held, loc, zs, zr, ms, mr)
    g = Reduction(place, G_STREAMS, *gs)
    c = Reduction(place, C_STREAMS, *cs)
    sketch = pltpu.make_async_copy(sk_ref, omega, osem.at[0])
    sketch.start()
    for sub in range(SUBS):
        rows.own(sub).start()
    greet(place)
    for sub in range(SUBS):
        for d in (2, 1, 3):
            rows.across(d, sub).start()
        rows.passing(0, sub, core).start()
    weights_into(place, len_ref, wcol)
    g.acc[...] = jnp.zeros_like(g.acc)
    c.acc[...] = jnp.zeros_like(c.acc)
    sketch.wait()
    step = rows.step

    def project(sub, k, which):
        x = jnp.concatenate([held[which, z, pl.ds(sub * step, step)] for z in range(4)], 1)
        prod = jnp.dot(x, omega[...], preferred_element_type=F32)
        w = wcol[which, pl.ds(sub * step, step)]
        s = prod * jnp.concatenate([w] * (omega.shape[1] // 128), 1)
        hi = s.astype(BF16)
        at = pl.ds((2 * sub + k) * step, step)
        sh[at] = hi
        sl[at] = (s - hi.astype(F32)).astype(BF16)

    def chunk(sub, _):
        rows.take(sub)
        project(sub, 0, core)
        rows.take_other(sub)
        project(sub, 1, 1 - core)
        at = pl.ds(2 * sub * step, 2 * step)
        for i in range(4):
            width = 128 * (i + 1)
            far = pl.ds(pl.multiple_of(core * width, 128), width)
            lh, ll, rh, rl = sh[at, 256 * i:256 * (i + 1)], sl[at, 256 * i:256 * (i + 1)], sh[at, far], sl[at, far]
            v = over_rows(lh, rh) + over_rows(lh, rl) + over_rows(ll, rh)
            half, lane = G_PLACES[i]
            g.acc[2 * half:2 * half + 2, :, :, :, lane:lane + width] += v.reshape(2, 4, 4, 8, width)
        return 0

    lax.fori_loop(0, SUBS, chunk, 0)
    for s in range(3):
        g.send(0, s)

    def cross(sub, _):
        mine = pl.ds(pl.multiple_of(core * 128, 128), 128)
        for k in range(2):
            which = core if k == 0 else 1 - core
            x = jnp.concatenate([held[which, z, pl.ds(sub * step, step), mine] for z in range(4)], 1)
            at = pl.ds((2 * sub + k) * step, step)
            v = over_rows(x, sh[at]) + over_rows(x, sl[at])
            c.acc[...] += v.reshape(4, 4, 4, 8, omega.shape[1])
        return 0

    lax.fori_loop(0, SUBS, cross, 0)
    sp = Spread(g, full, go_ref, ss, rs, fs, fr, ws)
    for s in range(3):
        g.gather(0, s)
        g.send(1, s)
    for s in range(3):
        c.send(0, s)
    for s in range(3):
        g.gather(1, s)
        g.share(s)
    for s in range(3):
        sp.seed(s)
        sp.send(1, s)
    for s in range(3):
        c.gather(0, s)
        c.send(1, s)
    for s in range(3):
        sp.wait(1, s)
        sp.send(2, s)
        sp.forward(s, 0)
    for s in range(3):
        c.gather(1, s)
        c.send(2, s)
    for d in (1, 3, 2):
        for s in range(3):
            sp.arrived(2, s, d)
            sp.forward(s, d)
    for s in range(3):
        c.gather(2, s)
        o, n = C_STREAMS[s]
        co_ref[0:8, o:o + n] = c.a[2][s][...]
    co_ref[8:16, :] = jnp.zeros((8, omega.shape[1]), F32)
    sp.finish()
    rows.finish()
    g.finish()
    c.finish()

def reduce_scratch(streams, last):
    lanes = sum(n for _, n in streams)
    def per(shape):
        return [pltpu.VMEM(shape + (8, n), F32) for _, n in streams]
    dma = pltpu.SemaphoreType.DMA
    return [pltpu.VMEM((4, 4, 4, 8, lanes), F32), per((3, 4, 4)), per((4, 4)), per((3, 4)), per((4,)), per((3,) + last), per(last),
            dma((3, 3, 3)), dma((3, 3, 3))]

def front(lengths, samples, sketch):
    dma = pltpu.SemaphoreType.DMA
    rows, feats = samples.shape
    width = sketch.shape[1]
    chunk = rows // 4
    return pl.pallas_call(
        front_kernel,
        out_shape=(jax.ShapeDtypeStruct((2, 4, 4, 4, 8, 640), F32), jax.ShapeDtypeStruct((16, width), F32)),
        in_specs=[pl.BlockSpec(memory_space=pltpu.SMEM), pl.BlockSpec(memory_space=pl.ANY), pl.BlockSpec(memory_space=pl.ANY)],
        out_specs=(pl.BlockSpec(memory_space=pl.ANY), pl.BlockSpec(memory_space=pltpu.VMEM)),
        scratch_shapes=[pltpu.VMEM((2, 4, chunk, feats), BF16), pltpu.VMEM(sketch.shape, BF16), pltpu.VMEM((2, chunk, 128), F32),
                        pltpu.VMEM((2 * chunk, width), BF16), pltpu.VMEM((2 * chunk, width), BF16),
                        reduce_scratch(G_STREAMS, (4,)), reduce_scratch(C_STREAMS, ()), pltpu.VMEM((2, 4, 4, 4, 8, 640), F32),
                        dma((3, 3, 3)), dma((3, 3, 3)), dma((3, 4)), dma((3, 4)), dma((3, 4, 2)),
                        dma((SUBS,)), dma((SUBS, 3)), dma((SUBS, 3)), dma((SUBS, 4)), dma((SUBS, 4)), dma((1,))],
        compiler_params=pltpu.CompilerParams(collective_id=1, has_side_effects=True, vmem_limit_bytes=56 << 20),
        cost_estimate=pl.CostEstimate(flops=13_000_000_000, bytes_accessed=8 << 20, transcendentals=0),
    )(lengths, samples.reshape(4, chunk, feats), sketch)

def swap_kernel(scale, y_ref, o_ref, got, flat, ssem, rsem):
    place = Place()
    tok = place.tok
    barrier = pltpu.get_barrier_semaphore()
    count = 32
    def hello(d, _):
        pl.semaphore_signal(barrier, inc=1, device_id=(lax.rem(tok + d, count), place.at[0]), device_id_type=MESH)
        return 0
    lax.fori_loop(1, count, hello, 0)
    pl.semaphore_wait(barrier, count - 1)
    def copy(d, owner):
        to = lax.rem(tok + d, count)
        lanes = pl.ds(pl.multiple_of((to // 4) * 128, 128), 128)
        return remote(y_ref.at[0:8, lanes], got.at[lax.rem(owner, 2), owner // 2], ssem.at[d], rsem.at[d], (to, place.at[0]))
    def start(d, _):
        copy(d, tok).start()
        return 0
    lax.fori_loop(1, count, start, 0)
    got[place.core, tok // 2] = y_ref[0:8, pl.ds(pl.multiple_of((tok // 4) * 128, 128), 128)]
    def done(d, _):
        copy(d, lax.rem(tok + count - d, count)).wait_recv()
        return 0
    lax.fori_loop(1, count, done, 0)
    for k in range(2):
        flat[:, 128 * k:128 * (k + 1)] = got[k].reshape(128, 128).T * scale
    o_ref[...] = flat[pl.ds(pl.multiple_of(lax.rem(tok, 4) * 32, 32), 32)]
    def sent(d, _):
        copy(d, tok).wait_send()
        return 0
    lax.fori_loop(1, count, sent, 0)

def swap(y, scale):
    dma = pltpu.SemaphoreType.DMA
    return pl.pallas_call(
        functools.partial(swap_kernel, scale),
        out_shape=jax.ShapeDtypeStruct((32, 256), F32),
        in_specs=[pl.BlockSpec(memory_space=pltpu.VMEM)],
        out_specs=pl.BlockSpec(memory_space=pltpu.VMEM),
        scratch_shapes=[pltpu.VMEM((2, 16, 8, 128), F32), pltpu.VMEM((128, 256), F32), dma((32,)), dma((32,))],
        compiler_params=pltpu.CompilerParams(collective_id=2, has_side_effects=True),
        cost_estimate=pl.CostEstimate(flops=0, bytes_accessed=1 << 20, transcendentals=0),
    )(y)

BLK = 128

def split(x):
    hi = x.astype(BF16)
    return hi, (x - hi.astype(F32)).astype(BF16)

def mm_t(a, b):
    return lax.dot_general(a, b, (((1,), (1,)), ((), ())), preferred_element_type=F32)

def mm3_t(a, b):
    (ah, al), (bh, bl) = a, b
    return mm_t(ah, bh) + (mm_t(ah, bl) + mm_t(al, bh))

def inverse_factor(m):
    n = m.shape[0]
    nb = n // 8
    sub = lax.broadcasted_iota(jnp.int32, (8, n), 0)
    lane = lax.broadcasted_iota(jnp.int32, (8, n), 1)
    row = lambda v, i: jnp.broadcast_to(v[i:i + 1], (8, n))
    col = lambda v, i: jnp.broadcast_to(v[:, i:i + 1], (8, n))
    z = [m[8 * q:8 * q + 8] for q in range(nb)]
    diag = [col(z[0], k) for k in range(8)]
    out = []
    for s in range(nb):
        at = 8 * s
        inside = (lane >= at) & (lane < at + 8)
        zs = jnp.where(inside, jnp.where(lane == at + sub, 1.0, 0.0), z[s])
        more = s + 1 < nb
        if more:
            below = [col(z[s + 1], at + k) for k in range(8)]
            ahead = [col(z[s + 1], at + 8 + k) for k in range(8)]
        l = [[None] * 8 for _ in range(8)]
        r, x, c = [], [], []
        w = None
        for k in range(8):
            r.append(lax.rsqrt(row(diag[k], k)))
            dk = diag[k] * r[k]
            for j in range(k + 1, 8):
                l[j][k] = row(diag[k], j) * r[k]
                diag[j] = diag[j] - dk * l[j][k]
            if more:
                ck = below[k]
                for j in range(k):
                    ck = ck - c[j] * l[k][j]
                c.append(ck * r[k])
                for j in range(8):
                    ahead[j] = ahead[j] - c[k] * row(c[k], j)
            xk = row(zs, k)
            for j in range(k):
                xk = xk - l[k][j] * x[j]
            x.append(xk * r[k])
            w = x[k] if w is None else jnp.where(sub == k, x[k], w)
        out.append(jnp.where(lane < at + 8, w, 0.0))
        if more:
            diag = ahead
            zq = jnp.where(inside, 0.0, z[s + 1])
            for k in range(8):
                zq = zq - c[k] * x[k]
            z[s + 1] = zq
        if s + 2 < nb:
            y = [None] * 8
            for k in range(7, -1, -1):
                yk = x[k]
                for i in range(7, k, -1):
                    yk = yk - l[i][k] * y[i]
                y[k] = yk * r[k]
            for q in range(s + 2, nb):
                zq = jnp.where(inside, 0.0, z[q])
                for k in range(7, -1, -1):
                    zq = zq - col(z[q], at + k) * y[k]
                z[q] = zq
    return jnp.concatenate(out, 0)
def chol_body(n, extra, e_ref, lh, ll):
    total = n + extra
    nb = n // BLK
    for b in range(nb):
        r0, r1 = b * BLK, (b + 1) * BLK
        w = split(inverse_factor(e_ref[r0:r1, r0:r1]))
        for c in range(b + 1, nb + 1):
            lo, hi = c * BLK, min((c + 1) * BLK, total)
            x = mm3_t(split(e_ref[lo:hi, r0:r1]), w)
            if c == nb:
                e_ref[lo:hi, r0:r1] = x
            xh, xl = split(x)
            lh[lo:hi, :] = xh
            ll[lo:hi, :] = xl
        for c in range(b + 1, nb):
            lo = c * BLK
            e_ref[lo:total, lo:lo + BLK] -= mm3_t((lh[lo:total], ll[lo:total]), (lh[lo:lo + BLK], ll[lo:lo + BLK]))

def unpack(g_ref, e, sem):
    copies = []
    for i, (half, lane) in enumerate(G_PLACES):
        width = 128 * (i + 1)
        for core in range(2):
            src = g_ref.at[core, 256 * half:256 * (half + 1), lane:lane + width]
            copies.append(pltpu.make_async_copy(src, e.at[256 * i:256 * (i + 1), core * width:(core + 1) * width], sem.at[2 * i + core]))
    return copies

def kernel(n, extra, g_ref, c_ref, o_ref, e, lh, ll, sem):
    copies = [pltpu.make_async_copy(c_ref, e.at[n:n + extra], sem.at[8])] + unpack(g_ref, e, sem)
    for c in copies:
        c.start()
    for c in copies:
        c.wait()
    chol_body(n, extra, e, lh, ll)
    o_ref[...] = e[n:n + extra, :]

def solve(g, ct, **kw):
    extra, n = ct.shape
    return pl.pallas_call(
        functools.partial(kernel, n, extra),
        out_shape=jax.ShapeDtypeStruct((extra, n), F32),
        in_specs=[pl.BlockSpec(memory_space=pl.ANY)] * 2,
        out_specs=pl.BlockSpec(memory_space=pltpu.VMEM),
        scratch_shapes=[pltpu.VMEM((n + extra, n), F32), pltpu.VMEM((n + extra, BLK), BF16), pltpu.VMEM((n + extra, BLK), BF16), pltpu.SemaphoreType.DMA((9,))],
        compiler_params=pltpu.CompilerParams(vmem_limit_bytes=60 << 20),
        cost_estimate=pl.CostEstimate(flops=2_000_000_000, bytes_accessed=8 << 20, transcendentals=1024),
        **kw,
    )(g, ct)


def shards(samples, lengths, sketch):
    total, mine = front(lengths, samples, sketch)
    y = solve(total.reshape(2, 512, 640), mine)
    scale = math.sqrt(sketch.shape[1] / (samples.shape[0] // 2 * lax.axis_size("tok")))
    return swap(y, scale)


def solution(mesh):
    in_specs = (P("tok", "col"), P(), P())
    out_specs = P("tok", "col")
    return jax.shard_map(shards, mesh=mesh, in_specs=in_specs, out_specs=out_specs, check_vma=False)
```

```python
import functools
import math

import jax
import jax.numpy as jnp
from jax import lax
from jax.experimental import pallas as pl
from jax.experimental.pallas import tpu as pltpu
from jax.sharding import PartitionSpec as P

F32, BF16 = jnp.float32, jnp.bfloat16
MESH = pl.DeviceIdType.MESH
G_STREAMS = ((0, 256), (256, 256), (512, 128))
C_STREAMS = ((0, 256), (256, 384), (640, 384))
G_PLACES = ((0, 512), (1, 384), (1, 0), (0, 0))
SUBS = 4
TOKS = 32
BLK = 128

class Place:
    def __init__(self):
        self.tok = lax.axis_index("tok")
        self.core = lax.rem(self.tok, 2)
        self.at = (lax.axis_index("col"), self.tok // 8, lax.rem(self.tok // 2, 4))

    def device(self, at, core):
        z, y, x = at
        return ((y * 4 + x) * 2 + core, z)

    def mate(self):
        return self.device(self.at, 1 - self.core)

    def peer(self, axis, d):
        at = list(self.at)
        at[axis] = lax.rem(at[axis] + d, 4)
        return self.device(at, self.core)

    def step(self, axis, d):
        return lax.rem(self.at[axis] + d + 4, 4)

def remote(src, dst, ssem, rsem, dev):
    return pltpu.make_async_remote_copy(src_ref=src, dst_ref=dst, send_sem=ssem, recv_sem=rsem, device_id=dev, device_id_type=MESH)

def pick(axis, p, lanes):
    idx = [slice(None)] * 3
    idx[axis] = p
    return tuple(idx) + (slice(None), pl.ds(*lanes))

def greet(place):
    barrier = pltpu.get_barrier_semaphore()
    def hello(d, _):
        pl.semaphore_signal(barrier, inc=1, device_id=(lax.rem(place.tok + d, TOKS), place.at[0]), device_id_type=MESH)
        return 0
    lax.fori_loop(1, TOKS, hello, 0)
    for d in range(1, 4):
        pl.semaphore_signal(barrier, inc=1, device_id=place.peer(0, d), device_id_type=MESH)
    pl.semaphore_wait(barrier, TOKS + 2)

class Reduction:
    def __init__(self, place, streams, acc, r1, a1, r2, a2, r3, a3, ps, pr):
        self.place, self.streams = place, streams
        self.acc, self.r, self.a = acc, (r1, r2, r3), (a1, a2, a3)
        self.ps, self.pr = ps, pr
        self.copies = {}

    def order(self, s):
        return (s, (s + 1) % 3, (s + 2) % 3)

    def sub(self, s, phase, p):
        if phase == 0:
            return pick(s, p, self.streams[s])
        if phase == 1 and s == 1:
            return (slice(None), p)
        return (p,)

    def source(self, s, phase):
        return self.acc if phase == 0 else self.a[phase - 1][s]

    def send(self, phase, s):
        axis = self.order(s)[phase]
        for d in (2, 1, 3):
            src = self.source(s, phase).at[self.sub(s, phase, self.place.step(axis, d))]
            c = remote(src, self.r[phase][s].at[d - 1], self.ps.at[phase, s, d - 1], self.pr.at[phase, s, d - 1], self.place.peer(axis, d))
            c.start()
            self.copies[phase, s, d] = c

    def gather(self, phase, s):
        axis = self.order(s)[phase]
        total = self.source(s, phase)[self.sub(s, phase, self.place.step(axis, 0))]
        for d in range(1, 4):
            self.copies[phase, s, d].wait_recv()
        r = self.r[phase][s]
        self.a[phase][s][...] = (total + r[0]) + (r[1] + r[2])

    def share(self, s):
        axis = self.order(s)[2]
        for d in (2, 1, 3):
            c = remote(self.a[1][s], self.r[2][s].at[d - 1], self.ps.at[2, s, d - 1], self.pr.at[2, s, d - 1], self.place.peer(axis, d))
            c.start()
            self.copies[2, s, d] = c

    def shared(self, s):
        for d in range(1, 4):
            self.copies[2, s, d].wait_recv()
        r = self.r[2][s]
        return (self.a[1][s][...] + r[0]) + (r[1] + r[2])

    def finish(self):
        for c in self.copies.values():
            c.wait_send()

class Spread:
    def __init__(self, red, full, ss, rs, fs, fr):
        self.red, self.full, self.place = red, full, red.place
        self.ss, self.rs, self.fs, self.fr = ss, rs, fs, fr
        self.sends = []

    def region(self, s, fixed, core):
        idx = [slice(None)] * 3
        for axis, p in fixed.items():
            idx[axis] = p
        return self.full.at[(core,) + tuple(idx) + (slice(None), pl.ds(*self.red.streams[s]))]

    def seed(self, s):
        idx = [slice(None)] * 3
        for axis in self.red.order(s)[:2]:
            idx[axis] = self.place.at[axis]
        o, n = self.red.streams[s]
        self.full[(self.place.core,) + tuple(idx) + (slice(None), slice(o, o + n))] = self.red.shared(s)

    def fixed(self, s, phase, d):
        axes = self.red.order(s)[:3 - phase]
        f = {a: self.place.at[a] for a in axes}
        f[axes[-1]] = self.place.step(axes[-1], -d)
        return f, axes[-1]

    def copy(self, phase, s, d, held):
        f, axis = self.fixed(s, phase, held)
        reg = self.region(s, f, self.place.core)
        return remote(reg, reg, self.ss.at[phase, s, d - 1], self.rs.at[phase, s, d - 1], self.place.peer(axis, d))

    def send(self, phase, s):
        for d in (2, 1, 3):
            c = self.copy(phase, s, d, 0)
            c.start()
            self.sends.append(c)

    def arrived(self, phase, s, d):
        self.copy(phase, s, d, d).wait_recv()

    def wait(self, phase, s):
        for d in range(1, 4):
            self.arrived(phase, s, d)

    def passing(self, s, d, core):
        f, _ = self.fixed(s, 2, d)
        reg = self.region(s, f, core)
        return remote(reg, reg, self.fs.at[s, d], self.fr.at[s, d], self.place.mate())

    def forward(self, s, d):
        c = self.passing(s, d, self.place.core)
        c.start()
        self.sends.append(c)

    def finish(self):
        for d in (0, 1, 3, 2):
            for s in range(3):
                self.passing(s, d, 1 - self.place.core).wait_recv()

    def sent(self):
        for c in self.sends:
            c.wait_send()

class Rows:
    def __init__(self, place, x, held, loc, zs, zr, ms, mr):
        self.place, self.x, self.held = place, x, held
        self.loc, self.zs, self.zr, self.ms, self.mr = loc, zs, zr, ms, mr
        self.step = held.shape[2] // SUBS

    def rows(self, sub):
        return pl.ds(sub * self.step, self.step)

    def slot(self, core, d, sub):
        return self.held.at[core, self.place.step(0, -d), self.rows(sub)]

    def own(self, sub):
        return pltpu.make_async_copy(self.x.at[self.place.at[0], self.rows(sub)], self.slot(self.place.core, 0, sub), self.loc.at[sub])

    def across(self, d, sub):
        return remote(self.x.at[self.place.step(0, d), self.rows(sub)], self.slot(self.place.core, 0, sub),
                      self.zs.at[sub, d - 1], self.zr.at[sub, d - 1], self.place.peer(0, d))

    def passing(self, d, sub, core):
        src = self.x.at[self.place.at[0], self.rows(sub)] if d == 0 else self.slot(core, d, sub)
        return remote(src, self.slot(core, d, sub), self.ms.at[sub, d], self.mr.at[sub, d], self.place.mate())

    def take(self, sub):
        self.own(sub).wait()
        for d in (1, 3, 2):
            remote(self.slot(self.place.core, d, sub), self.slot(self.place.core, d, sub),
                   self.zs.at[sub, d - 1], self.zr.at[sub, d - 1], self.place.peer(0, d)).wait_recv()
            self.passing(d, sub, self.place.core).start()

    def take_other(self, sub):
        for d in range(4):
            self.passing(d, sub, 1 - self.place.core).wait_recv()

    def finish(self):
        for sub in range(SUBS):
            for d in range(4):
                self.passing(d, sub, self.place.core).wait_send()
                if d:
                    self.across(d, sub).wait_send()

def over_rows(a, b):
    return lax.dot_general(a, b, (((0,), (0,)), ((), ())), preferred_element_type=F32)

def weights_into(place, lengths, wcol):
    rows = wcol.shape[1]
    assert rows == 1024
    pos = place.at[0] * rows + lax.broadcasted_iota(jnp.int32, (8, 128), 0) * 128 + lax.broadcasted_iota(jnp.int32, (8, 128), 1)
    for k in range(2):
        buf = place.tok - place.core + k
        start = jnp.zeros((8, 128), jnp.int32)
        w = jnp.zeros((8, 128), F32)
        for s in range(lengths.shape[1]):
            count = jnp.full((8, 128), lengths[buf, s], jnp.int32)
            per = lax.rsqrt(1.0 + 4.0 * count.astype(F32) / float(2 * rows))
            w = w + jnp.where((pos >= start) & (pos < start + count), per, 0.0)
            start = start + count
        wt = w.T
        for a in range(8):
            wcol[k, 128 * a:128 * (a + 1)] = jnp.broadcast_to(wt[:, a:a + 1], (128, 128))

def whole_kernel(scale, len_ref, x_ref, sk_ref, o_ref, held, omega, wcol, sh, sl, gs, cs, full, ext, lh, ll, wh, wl, got, flat, ss, rs, fs, fr, loc, zs, zr, ms, mr, osem, ys, yr):
    place = Place()
    core = place.core
    rows = Rows(place, x_ref, held, loc, zs, zr, ms, mr)
    g = Reduction(place, G_STREAMS, *gs)
    c = Reduction(place, C_STREAMS, *cs)
    sketch = pltpu.make_async_copy(sk_ref, omega, osem.at[0])
    sketch.start()
    for sub in range(SUBS):
        rows.own(sub).start()
    greet(place)
    for sub in range(SUBS):
        for d in (2, 1, 3):
            rows.across(d, sub).start()
        rows.passing(0, sub, core).start()
    weights_into(place, len_ref, wcol)
    g.acc[...] = jnp.zeros_like(g.acc)
    c.acc[...] = jnp.zeros_like(c.acc)
    sketch.wait()
    step = rows.step

    def project(sub, k, which):
        x = jnp.concatenate([held[which, z, pl.ds(sub * step, step)] for z in range(4)], 1)
        prod = jnp.dot(x, omega[...], preferred_element_type=F32)
        w = wcol[which, pl.ds(sub * step, step)]
        s = prod * jnp.concatenate([w] * (omega.shape[1] // 128), 1)
        hi = s.astype(BF16)
        at = pl.ds((2 * sub + k) * step, step)
        sh[at] = hi
        sl[at] = (s - hi.astype(F32)).astype(BF16)

    def chunk(sub, _):
        rows.take(sub)
        project(sub, 0, core)
        rows.take_other(sub)
        project(sub, 1, 1 - core)
        at = pl.ds(2 * sub * step, 2 * step)
        for i in range(4):
            width = 128 * (i + 1)
            far = pl.ds(pl.multiple_of(core * width, 128), width)
            lh, ll, rh, rl = sh[at, 256 * i:256 * (i + 1)], sl[at, 256 * i:256 * (i + 1)], sh[at, far], sl[at, far]
            v = over_rows(lh, rh) + over_rows(lh, rl) + over_rows(ll, rh)
            half, lane = G_PLACES[i]
            g.acc[2 * half:2 * half + 2, :, :, :, lane:lane + width] += v.reshape(2, 4, 4, 8, width)
        return 0

    lax.fori_loop(0, SUBS, chunk, 0)
    for s in range(3):
        g.send(0, s)

    def cross(sub, _):
        mine = pl.ds(pl.multiple_of(core * 128, 128), 128)
        for k in range(2):
            which = core if k == 0 else 1 - core
            x = jnp.concatenate([held[which, z, pl.ds(sub * step, step), mine] for z in range(4)], 1)
            at = pl.ds((2 * sub + k) * step, step)
            v = over_rows(x, sh[at]) + over_rows(x, sl[at])
            c.acc[...] += v.reshape(4, 4, 4, 8, omega.shape[1])
        return 0

    lax.fori_loop(0, SUBS, cross, 0)
    sp = Spread(g, full, ss, rs, fs, fr)
    for s in range(3):
        g.gather(0, s)
        g.send(1, s)
    for s in range(3):
        g.gather(1, s)
        g.share(s)
    for s in range(3):
        sp.seed(s)
        sp.send(1, s)
    for s in range(3):
        sp.wait(1, s)
        sp.send(2, s)
        sp.forward(s, 0)
    for s in range(3):
        c.send(0, s)
    for d in (1, 3, 2):
        for s in range(3):
            sp.arrived(2, s, d)
            sp.forward(s, d)
    sp.finish()
    sp.sent()

    result = Result(place, ext, got, flat, ys, yr)

    def meanwhile(b):
        if b == 2:
            for s in range(3):
                c.gather(0, s)
                c.send(1, s)
        if b == 3:
            for s in range(3):
                c.gather(1, s)
                c.send(2, s)
        if b == 5:
            for s in range(3):
                c.gather(2, s)
                o, n = C_STREAMS[s]
                ext[0:8, o:o + n] = c.a[2][s][...]
            ext[8:16, :] = jnp.zeros((8, omega.shape[1]), F32)
        if b >= 5:
            for k in range(0 if b == 5 else b, b + 1):
                extend(k, ext, lh, ll, wh, wl)
                result.send(k)

    factor(full, lh, ll, wh, wl, meanwhile)
    result.finish(o_ref, scale)
    rows.finish()
    g.finish()
    c.finish()

def reduce_scratch(streams, last):
    lanes = sum(n for _, n in streams)
    def per(shape):
        return [pltpu.VMEM(shape + (8, n), F32) for _, n in streams]
    dma = pltpu.SemaphoreType.DMA
    return [pltpu.VMEM((4, 4, 4, 8, lanes), F32), per((3, 4, 4)), per((4, 4)), per((3, 4)), per((4,)), per((3,) + last), per(last),
            dma((3, 3, 3)), dma((3, 3, 3))]

class Result:
    def __init__(self, place, ext, got, flat, ys, yr):
        self.place, self.ext, self.got, self.flat, self.ys, self.yr = place, ext, got, flat, ys, yr

    def copy(self, to, owner, b):
        return remote(self.ext.at[0:8, BLK * b:BLK * (b + 1)], self.got.at[lax.rem(owner, 2), owner // 2], self.ys.at[to], self.yr.at[owner], (to, self.place.at[0]))

    def send(self, b):
        tok = self.place.tok
        for to in range(4 * b, 4 * b + 4):
            @pl.when(tok != to)
            def _():
                self.copy(to, tok, b).start()
        @pl.when(tok // 4 == b)
        def _():
            self.got[self.place.core, tok // 2] = self.ext[0:8, BLK * b:BLK * (b + 1)]

    def finish(self, o_ref, scale):
        tok = self.place.tok
        def landed(d, _):
            src = lax.rem(tok + d, TOKS)
            self.copy(src, src, 0).wait_recv()
            return 0
        lax.fori_loop(1, TOKS, landed, 0)
        for k in range(2):
            self.flat[:, 128 * k:128 * (k + 1)] = self.got[k].reshape(128, 128).T * scale
        o_ref[...] = self.flat[pl.ds(pl.multiple_of(lax.rem(tok, 4) * 32, 32), 32)]
        def sent(d, _):
            self.copy(lax.rem(tok + d, TOKS), tok, 0).wait_send()
            return 0
        lax.fori_loop(1, TOKS, sent, 0)

def split(x):
    hi = x.astype(BF16)
    return hi, (x - hi.astype(F32)).astype(BF16)

def mm_t(a, b):
    return lax.dot_general(a, b, (((1,), (1,)), ((), ())), preferred_element_type=F32)

def mm3_t(a, b):
    (ah, al), (bh, bl) = a, b
    return mm_t(ah, bh) + (mm_t(ah, bl) + mm_t(al, bh))

def inverse_factor(m):
    n = m.shape[0]
    nb = n // 8
    sub = lax.broadcasted_iota(jnp.int32, (8, n), 0)
    lane = lax.broadcasted_iota(jnp.int32, (8, n), 1)
    row = lambda v, i: jnp.broadcast_to(v[i:i + 1], (8, n))
    col = lambda v, i: jnp.broadcast_to(v[:, i:i + 1], (8, n))
    z = [m[8 * q:8 * q + 8] for q in range(nb)]
    diag = [col(z[0], k) for k in range(8)]
    out = []
    for s in range(nb):
        at = 8 * s
        inside = (lane >= at) & (lane < at + 8)
        zs = jnp.where(inside, jnp.where(lane == at + sub, 1.0, 0.0), z[s])
        more = s + 1 < nb
        if more:
            below = [col(z[s + 1], at + k) for k in range(8)]
            ahead = [col(z[s + 1], at + 8 + k) for k in range(8)]
        l = [[None] * 8 for _ in range(8)]
        r, x, c = [], [], []
        w = None
        for k in range(8):
            r.append(lax.rsqrt(row(diag[k], k)))
            dk = diag[k] * r[k]
            for j in range(k + 1, 8):
                l[j][k] = row(diag[k], j) * r[k]
                diag[j] = diag[j] - dk * l[j][k]
            if more:
                ck = below[k]
                for j in range(k):
                    ck = ck - c[j] * l[k][j]
                c.append(ck * r[k])
                for j in range(8):
                    ahead[j] = ahead[j] - c[k] * row(c[k], j)
            xk = row(zs, k)
            for j in range(k):
                xk = xk - l[k][j] * x[j]
            x.append(xk * r[k])
            w = x[k] if w is None else jnp.where(sub == k, x[k], w)
        out.append(jnp.where(lane < at + 8, w, 0.0))
        if more:
            diag = ahead
            zq = jnp.where(inside, 0.0, z[s + 1])
            for k in range(8):
                zq = zq - c[k] * x[k]
            z[s + 1] = zq
        if s + 2 < nb:
            y = [None] * 8
            for k in range(7, -1, -1):
                yk = x[k]
                for i in range(7, k, -1):
                    yk = yk - l[i][k] * y[i]
                y[k] = yk * r[k]
            for q in range(s + 2, nb):
                zq = jnp.where(inside, 0.0, z[q])
                for k in range(7, -1, -1):
                    zq = zq - col(z[q], at + k) * y[k]
                z[q] = zq
    return jnp.concatenate(out, 0)
def block(r, c):
    i = r // 2
    width = 128 * (i + 1)
    core = (128 * c) // width
    half, lane = G_PLACES[i]
    lane += 128 * c - core * width
    return (core, 2 * half + r % 2, slice(None), slice(None), slice(None), slice(lane, lane + BLK))

def factor(full, lh, ll, wh, wl, meanwhile):
    nb = wh.shape[0]
    get = lambda r, c: full[block(r, c)].reshape(BLK, BLK)
    for b in range(nb):
        w = split(inverse_factor(get(b, b)))
        wh[b], wl[b] = w
        for r in range(b + 1, nb):
            at = slice(r * BLK, (r + 1) * BLK)
            lh[b, at], ll[b, at] = split(mm3_t(split(get(r, b)), w))
        for c in range(b + 1, nb):
            below, at = slice(c * BLK, nb * BLK), slice(c * BLK, (c + 1) * BLK)
            v = mm3_t((lh[b, below], ll[b, below]), (lh[b, at], ll[b, at]))
            for r in range(c, nb):
                idx = block(r, c)
                full[idx] = full[idx] - v[(r - c) * BLK:(r - c + 1) * BLK].reshape(4, 4, 8, BLK)
        meanwhile(b)

def extend(b, ext, lh, ll, wh, wl):
    at, rest = slice(b * BLK, (b + 1) * BLK), slice((b + 1) * BLK, ext.shape[1])
    y = mm3_t(split(ext[:, at]), (wh[b], wl[b]))
    ext[:, at] = y
    if rest.start < rest.stop:
        ext[:, rest] = ext[:, rest] - mm3_t(split(y), (lh[b, rest], ll[b, rest]))

def whole(lengths, samples, sketch, scale):
    dma = pltpu.SemaphoreType.DMA
    rows, feats = samples.shape
    width = sketch.shape[1]
    chunk = rows // 4
    nb = width // BLK
    return pl.pallas_call(
        functools.partial(whole_kernel, scale),
        out_shape=jax.ShapeDtypeStruct((width // TOKS, feats), F32),
        in_specs=[pl.BlockSpec(memory_space=pltpu.SMEM), pl.BlockSpec(memory_space=pl.ANY), pl.BlockSpec(memory_space=pl.ANY)],
        out_specs=pl.BlockSpec(memory_space=pltpu.VMEM),
        scratch_shapes=[pltpu.VMEM((2, 4, chunk, feats), BF16), pltpu.VMEM(sketch.shape, BF16), pltpu.VMEM((2, chunk, 128), F32),
                        pltpu.VMEM((2 * chunk, width), BF16), pltpu.VMEM((2 * chunk, width), BF16),
                        reduce_scratch(G_STREAMS, (4,)), reduce_scratch(C_STREAMS, ()), pltpu.VMEM((2, 4, 4, 4, 8, 640), F32),
                        pltpu.VMEM((16, width), F32), pltpu.VMEM((nb, width, BLK), BF16), pltpu.VMEM((nb, width, BLK), BF16),
                        pltpu.VMEM((nb, BLK, BLK), BF16), pltpu.VMEM((nb, BLK, BLK), BF16),
                        pltpu.VMEM((2, 16, 8, BLK), F32), pltpu.VMEM((BLK, feats), F32),
                        dma((3, 3, 3)), dma((3, 3, 3)), dma((3, 4)), dma((3, 4)),
                        dma((SUBS,)), dma((SUBS, 3)), dma((SUBS, 3)), dma((SUBS, 4)), dma((SUBS, 4)), dma((1,)),
                        dma((TOKS,)), dma((TOKS,))],
        compiler_params=pltpu.CompilerParams(collective_id=1, has_side_effects=True, vmem_limit_bytes=60 << 20),
        cost_estimate=pl.CostEstimate(flops=15_000_000_000, bytes_accessed=8 << 20, transcendentals=0),
    )(lengths, samples.reshape(4, chunk, feats), sketch)


def shards(samples, lengths, sketch):
    scale = math.sqrt(sketch.shape[1] / (samples.shape[0] // 2 * lax.axis_size("tok")))
    return whole(lengths, samples, sketch, scale)


def solution(mesh):
    in_specs = (P("tok", "col"), P(), P())
    out_specs = P("tok", "col")
    return jax.shard_map(shards, mesh=mesh, in_specs=in_specs, out_specs=out_specs, check_vma=False)
```

```python
import functools
import math

import jax
import jax.numpy as jnp
from jax import lax
from jax.experimental import pallas as pl
from jax.experimental.pallas import tpu as pltpu
from jax.sharding import PartitionSpec as P

F32, BF16 = jnp.float32, jnp.bfloat16
MESH = pl.DeviceIdType.MESH
G_STREAMS = ((0, 256), (256, 256), (512, 128))
C_STREAMS = ((0, 256), (256, 384), (640, 384))
G_PLACES = ((0, 512), (1, 384), (1, 0), (0, 0))
SUBS = 8
TOKS = 32
BLK = 128

class Place:
    def __init__(self):
        self.tok = lax.axis_index("tok")
        self.core = lax.rem(self.tok, 2)
        self.at = (lax.axis_index("col"), self.tok // 8, lax.rem(self.tok // 2, 4))

    def device(self, at, core):
        z, y, x = at
        return ((y * 4 + x) * 2 + core, z)

    def mate(self):
        return self.device(self.at, 1 - self.core)

    def peer(self, axis, d):
        at = list(self.at)
        at[axis] = lax.rem(at[axis] + d, 4)
        return self.device(at, self.core)

    def step(self, axis, d):
        return lax.rem(self.at[axis] + d + 4, 4)

def remote(src, dst, ssem, rsem, dev):
    return pltpu.make_async_remote_copy(src_ref=src, dst_ref=dst, send_sem=ssem, recv_sem=rsem, device_id=dev, device_id_type=MESH)

def pick(axis, p, lanes):
    idx = [slice(None)] * 3
    idx[axis] = p
    return tuple(idx) + (slice(None), pl.ds(*lanes))

def greet(place):
    barrier = pltpu.get_barrier_semaphore()
    def hello(d, _):
        pl.semaphore_signal(barrier, inc=1, device_id=(lax.rem(place.tok + d, TOKS), place.at[0]), device_id_type=MESH)
        return 0
    lax.fori_loop(1, TOKS, hello, 0)
    for d in range(1, 4):
        pl.semaphore_signal(barrier, inc=1, device_id=place.peer(0, d), device_id_type=MESH)
    pl.semaphore_wait(barrier, TOKS + 2)

class Reduction:
    def __init__(self, place, streams, acc, r1, a1, r2, a2, r3, a3, ps, pr):
        self.place, self.streams = place, streams
        self.acc, self.r, self.a = acc, (r1, r2, r3), (a1, a2, a3)
        self.ps, self.pr = ps, pr
        self.copies = {}

    def order(self, s):
        return (s, (s + 1) % 3, (s + 2) % 3)

    def sub(self, s, phase, p):
        if phase == 0:
            return pick(s, p, self.streams[s])
        if phase == 1 and s == 1:
            return (slice(None), p)
        return (p,)

    def source(self, s, phase):
        return self.acc if phase == 0 else self.a[phase - 1][s]

    def send(self, phase, s):
        axis = self.order(s)[phase]
        for d in (2, 1, 3):
            src = self.source(s, phase).at[self.sub(s, phase, self.place.step(axis, d))]
            c = remote(src, self.r[phase][s].at[d - 1], self.ps.at[phase, s, d - 1], self.pr.at[phase, s, d - 1], self.place.peer(axis, d))
            c.start()
            self.copies[phase, s, d] = c

    def gather(self, phase, s):
        axis = self.order(s)[phase]
        total = self.source(s, phase)[self.sub(s, phase, self.place.step(axis, 0))]
        for d in range(1, 4):
            self.copies[phase, s, d].wait_recv()
        r = self.r[phase][s]
        self.a[phase][s][...] = (total + r[0]) + (r[1] + r[2])

    def share(self, s):
        axis = self.order(s)[2]
        for d in (2, 1, 3):
            c = remote(self.a[1][s], self.r[2][s].at[d - 1], self.ps.at[2, s, d - 1], self.pr.at[2, s, d - 1], self.place.peer(axis, d))
            c.start()
            self.copies[2, s, d] = c

    def shared(self, s):
        for d in range(1, 4):
            self.copies[2, s, d].wait_recv()
        r = self.r[2][s]
        return (self.a[1][s][...] + r[0]) + (r[1] + r[2])

    def finish(self):
        for c in self.copies.values():
            c.wait_send()

class Spread:
    def __init__(self, red, full, ss, rs, fs, fr):
        self.red, self.full, self.place = red, full, red.place
        self.ss, self.rs, self.fs, self.fr = ss, rs, fs, fr
        self.sends = []

    def region(self, s, fixed, core):
        idx = [slice(None)] * 3
        for axis, p in fixed.items():
            idx[axis] = p
        return self.full.at[(core,) + tuple(idx) + (slice(None), pl.ds(*self.red.streams[s]))]

    def seed(self, s):
        idx = [slice(None)] * 3
        for axis in self.red.order(s)[:2]:
            idx[axis] = self.place.at[axis]
        o, n = self.red.streams[s]
        self.full[(self.place.core,) + tuple(idx) + (slice(None), slice(o, o + n))] = self.red.shared(s)

    def fixed(self, s, phase, d):
        axes = self.red.order(s)[:3 - phase]
        f = {a: self.place.at[a] for a in axes}
        f[axes[-1]] = self.place.step(axes[-1], -d)
        return f, axes[-1]

    def copy(self, phase, s, d, held):
        f, axis = self.fixed(s, phase, held)
        reg = self.region(s, f, self.place.core)
        return remote(reg, reg, self.ss.at[phase, s, d - 1], self.rs.at[phase, s, d - 1], self.place.peer(axis, d))

    def send(self, phase, s):
        for d in (2, 1, 3):
            c = self.copy(phase, s, d, 0)
            c.start()
            self.sends.append(c)

    def arrived(self, phase, s, d):
        self.copy(phase, s, d, d).wait_recv()

    def wait(self, phase, s):
        for d in range(1, 4):
            self.arrived(phase, s, d)

    def passing(self, s, d, core):
        f, _ = self.fixed(s, 2, d)
        reg = self.region(s, f, core)
        return remote(reg, reg, self.fs.at[s, d], self.fr.at[s, d], self.place.mate())

    def forward(self, s, d):
        c = self.passing(s, d, self.place.core)
        c.start()
        self.sends.append(c)

    def finish(self, s):
        for d in (0, 1, 3, 2):
            self.passing(s, d, 1 - self.place.core).wait_recv()

    def sent(self):
        for c in self.sends:
            c.wait_send()

class Rows:
    def __init__(self, place, x, held, loc, zs, zr, ms, mr):
        self.place, self.x, self.held = place, x, held
        self.loc, self.zs, self.zr, self.ms, self.mr = loc, zs, zr, ms, mr
        self.step = held.shape[2] // SUBS

    def rows(self, sub):
        return pl.ds(sub * self.step, self.step)

    def slot(self, core, d, sub):
        return self.held.at[core, self.place.step(0, -d), self.rows(sub)]

    def own(self, sub):
        return pltpu.make_async_copy(self.x.at[self.place.at[0], self.rows(sub)], self.slot(self.place.core, 0, sub), self.loc.at[sub])

    def across(self, d, sub):
        return remote(self.x.at[self.place.step(0, d), self.rows(sub)], self.slot(self.place.core, 0, sub),
                      self.zs.at[sub, d - 1], self.zr.at[sub, d - 1], self.place.peer(0, d))

    def passing(self, d, sub, core):
        src = self.x.at[self.place.at[0], self.rows(sub)] if d == 0 else self.slot(core, d, sub)
        return remote(src, self.slot(core, d, sub), self.ms.at[sub, d], self.mr.at[sub, d], self.place.mate())

    def take(self, sub):
        self.own(sub).wait()
        for d in (1, 3, 2):
            remote(self.slot(self.place.core, d, sub), self.slot(self.place.core, d, sub),
                   self.zs.at[sub, d - 1], self.zr.at[sub, d - 1], self.place.peer(0, d)).wait_recv()
            self.passing(d, sub, self.place.core).start()

    def take_other(self, sub):
        for d in range(4):
            self.passing(d, sub, 1 - self.place.core).wait_recv()

    def finish(self):
        for sub in range(SUBS):
            for d in range(4):
                self.passing(d, sub, self.place.core).wait_send()
                if d:
                    self.across(d, sub).wait_send()

def over_rows(a, b):
    return lax.dot_general(a, b, (((0,), (0,)), ((), ())), preferred_element_type=F32)

def weights_into(place, lengths, wcol):
    rows = wcol.shape[1]
    assert rows == 1024
    pos = place.at[0] * rows + lax.broadcasted_iota(jnp.int32, (8, 128), 0) * 128 + lax.broadcasted_iota(jnp.int32, (8, 128), 1)
    for k in range(2):
        own = lengths[pl.ds(place.tok - place.core + k, 1), :]
        start = jnp.zeros((8, 128), jnp.int32)
        w = jnp.zeros((8, 128), F32)
        for s in range(lengths.shape[1]):
            count = jnp.broadcast_to(own[:, s:s + 1], (8, 128))
            per = lax.rsqrt(1.0 + 4.0 * count.astype(F32) / float(2 * rows))
            w = w + jnp.where((pos >= start) & (pos < start + count), per, 0.0)
            start = start + count
        wt = w.T
        for a in range(8):
            wcol[k, 128 * a:128 * (a + 1)] = jnp.broadcast_to(wt[:, a:a + 1], (128, 128))

def whole_kernel(scale, len_ref, x_ref, sk_ref, o_ref, held, omega, wcol, sh, sl, gs, cs, full, ext, lh, ll, wh, wl, got, flat, ss, rs, fs, fr, loc, zs, zr, ms, mr, osem, ys, yr):
    place = Place()
    core = place.core
    rows = Rows(place, x_ref, held, loc, zs, zr, ms, mr)
    g = Reduction(place, G_STREAMS, *gs)
    c = Reduction(place, C_STREAMS, *cs)
    sketch = pltpu.make_async_copy(sk_ref, omega, osem.at[0])
    sketch.start()
    for sub in range(SUBS):
        rows.own(sub).start()
    greet(place)
    for sub in range(SUBS):
        for d in (2, 1, 3):
            rows.across(d, sub).start()
        rows.passing(0, sub, core).start()
    weights_into(place, len_ref, wcol)
    g.acc[...] = jnp.zeros_like(g.acc)
    c.acc[...] = jnp.zeros_like(c.acc)
    sketch.wait()
    step = rows.step

    def project(sub, k, which):
        x = jnp.concatenate([held[which, z, pl.ds(sub * step, step)] for z in range(4)], 1)
        prod = jnp.dot(x, omega[...], preferred_element_type=F32)
        w = wcol[which, pl.ds(sub * step, step)]
        s = prod * jnp.concatenate([w] * (omega.shape[1] // 128), 1)
        hi = s.astype(BF16)
        at = pl.ds((2 * sub + k) * step, step)
        sh[at] = hi
        sl[at] = (s - hi.astype(F32)).astype(BF16)

    def chunk(sub, _):
        rows.take(sub)
        project(sub, 0, core)
        rows.take_other(sub)
        project(sub, 1, 1 - core)
        at = pl.ds(2 * sub * step, 2 * step)
        for i in range(4):
            width = 128 * (i + 1)
            far = pl.ds(pl.multiple_of(core * width, 128), width)
            lh, ll, rh, rl = sh[at, 256 * i:256 * (i + 1)], sl[at, 256 * i:256 * (i + 1)], sh[at, far], sl[at, far]
            v = over_rows(lh, rh) + over_rows(lh, rl) + over_rows(ll, rh)
            half, lane = G_PLACES[i]
            g.acc[2 * half:2 * half + 2, :, :, :, lane:lane + width] += v.reshape(2, 4, 4, 8, width)
        return 0

    lax.fori_loop(0, SUBS, chunk, 0)
    for s in range(3):
        g.send(0, s)

    def cross(sub, _):
        mine = pl.ds(pl.multiple_of(core * 128, 128), 128)
        x = jnp.concatenate([
            jnp.concatenate([held[which, z, pl.ds(sub * step, step), mine] for z in range(4)], 1) for which in (core, 1 - core)], 0)
        at = pl.ds(2 * sub * step, 2 * step)
        v = over_rows(x, sh[at]) + over_rows(x, sl[at])
        c.acc[...] += v.reshape(4, 4, 4, 8, omega.shape[1])
        return 0

    lax.fori_loop(0, SUBS, cross, 0)
    sp = Spread(g, full, ss, rs, fs, fr)
    for s in range(3):
        g.gather(0, s)
        g.send(1, s)
    for s in range(3):
        c.send(0, s)
    for s in range(3):
        g.gather(1, s)
        g.share(s)
    for s in range(3):
        sp.seed(s)
        sp.send(1, s)
    for s in range(3):
        sp.wait(1, s)
        sp.send(2, s)
        sp.forward(s, 0)
    for s in range(3):
        c.gather(0, s)
        c.send(1, s)
    for d in (1, 3, 2):
        for s in (2, 0, 1):
            sp.arrived(2, s, d)
            sp.forward(s, d)
    sp.finish(2)

    def settled():
        sp.finish(0)
        sp.finish(1)
        sp.sent()

    result = Result(place, ext, got, flat, ys, yr)

    def meanwhile(b):
        if b == 1:
            for s in range(3):
                c.gather(1, s)
                c.send(2, s)
        if b == 3:
            for s in range(3):
                c.gather(2, s)
                o, n = C_STREAMS[s]
                ext[0:8, o:o + n] = c.a[2][s][...]
            ext[8:16, :] = jnp.zeros((8, omega.shape[1]), F32)
        if b >= 3:
            for k in range(0 if b == 3 else b, b + 1):
                extend(k, ext, lh, ll, wh, wl)
                result.send(k)

    factor(full, lh, ll, wh, wl, settled, meanwhile)
    result.finish(o_ref, scale)
    rows.finish()
    g.finish()
    c.finish()

def reduce_scratch(streams, last):
    lanes = sum(n for _, n in streams)
    def per(shape):
        return [pltpu.VMEM(shape + (8, n), F32) for _, n in streams]
    dma = pltpu.SemaphoreType.DMA
    return [pltpu.VMEM((4, 4, 4, 8, lanes), F32), per((3, 4, 4)), per((4, 4)), per((3, 4)), per((4,)), per((3,) + last), per(last),
            dma((3, 3, 3)), dma((3, 3, 3))]

class Result:
    def __init__(self, place, ext, got, flat, ys, yr):
        self.place, self.ext, self.got, self.flat, self.ys, self.yr = place, ext, got, flat, ys, yr

    def copy(self, to, owner, b):
        return remote(self.ext.at[0:8, BLK * b:BLK * (b + 1)], self.got.at[lax.rem(owner, 2), owner // 2], self.ys.at[to], self.yr.at[owner], (to, self.place.at[0]))

    def send(self, b):
        tok = self.place.tok
        for to in range(4 * b, 4 * b + 4):
            @pl.when(tok != to)
            def _():
                self.copy(to, tok, b).start()
        @pl.when(tok // 4 == b)
        def _():
            self.got[self.place.core, tok // 2] = self.ext[0:8, BLK * b:BLK * (b + 1)]

    def finish(self, o_ref, scale):
        tok = self.place.tok
        def landed(d, _):
            src = lax.rem(tok + d, TOKS)
            self.copy(src, src, 0).wait_recv()
            return 0
        lax.fori_loop(1, TOKS, landed, 0)
        for k in range(2):
            self.flat[:, 128 * k:128 * (k + 1)] = self.got[k].reshape(128, 128).T * scale
        o_ref[...] = self.flat[pl.ds(pl.multiple_of(lax.rem(tok, 4) * 32, 32), 32)]
        def sent(d, _):
            self.copy(lax.rem(tok + d, TOKS), tok, 0).wait_send()
            return 0
        lax.fori_loop(1, TOKS, sent, 0)

def split(x):
    hi = x.astype(BF16)
    return hi, (x - hi.astype(F32)).astype(BF16)

def mm_t(a, b):
    return lax.dot_general(a, b, (((1,), (1,)), ((), ())), preferred_element_type=F32)

def mm3_t(a, b):
    (ah, al), (bh, bl) = a, b
    return mm_t(ah, bh) + (mm_t(ah, bl) + mm_t(al, bh))

def inverse_factor(m):
    n = m.shape[0]
    nb = n // 8
    sub = lax.broadcasted_iota(jnp.int32, (8, n), 0)
    lane = lax.broadcasted_iota(jnp.int32, (8, n), 1)
    row = lambda v, i: jnp.broadcast_to(v[i:i + 1], (8, n))
    col = lambda v, i: jnp.broadcast_to(v[:, i:i + 1], (8, n))
    z = [m[8 * q:8 * q + 8] for q in range(nb)]
    diag = [col(z[0], k) for k in range(8)]
    out = []
    for s in range(nb):
        at = 8 * s
        inside = (lane >= at) & (lane < at + 8)
        zs = jnp.where(inside, jnp.where(lane == at + sub, 1.0, 0.0), z[s])
        more = s + 1 < nb
        if more:
            below = [col(z[s + 1], at + k) for k in range(8)]
            ahead = [col(z[s + 1], at + 8 + k) for k in range(8)]
        l = [[None] * 8 for _ in range(8)]
        r, x, c = [], [], []
        w = None
        for k in range(8):
            r.append(lax.rsqrt(row(diag[k], k)))
            dk = diag[k] * r[k]
            for j in range(k + 1, 8):
                l[j][k] = row(diag[k], j) * r[k]
                diag[j] = diag[j] - dk * l[j][k]
            if more:
                ck = below[k]
                for j in range(k):
                    ck = ck - c[j] * l[k][j]
                c.append(ck * r[k])
                for j in range(8):
                    ahead[j] = ahead[j] - c[k] * row(c[k], j)
            xk = row(zs, k)
            for j in range(k):
                xk = xk - l[k][j] * x[j]
            x.append(xk * r[k])
            w = x[k] if w is None else jnp.where(sub == k, x[k], w)
        out.append(jnp.where(lane < at + 8, w, 0.0))
        if more:
            diag = ahead
            zq = jnp.where(inside, 0.0, z[s + 1])
            for k in range(8):
                zq = zq - c[k] * x[k]
            z[s + 1] = zq
        if s + 2 < nb:
            y = [None] * 8
            for k in range(7, -1, -1):
                yk = x[k]
                for i in range(7, k, -1):
                    yk = yk - l[i][k] * y[i]
                y[k] = yk * r[k]
            for q in range(s + 2, nb):
                zq = jnp.where(inside, 0.0, z[q])
                for k in range(7, -1, -1):
                    zq = zq - col(z[q], at + k) * y[k]
                z[q] = zq
    return jnp.concatenate(out, 0)
def block(r, c):
    i = r // 2
    width = 128 * (i + 1)
    core = (128 * c) // width
    half, lane = G_PLACES[i]
    lane += 128 * c - core * width
    return (core, 2 * half + r % 2, slice(None), slice(None), slice(None), slice(lane, lane + BLK))

def factor(full, lh, ll, wh, wl, settled, meanwhile):
    nb = wh.shape[0]
    get = lambda r, c: full[block(r, c)].reshape(BLK, BLK)
    for b in range(nb):
        w = split(inverse_factor(get(b, b)))
        wh[b], wl[b] = w
        if b == 0:
            settled()
        for r in range(b + 1, nb):
            at = slice(r * BLK, (r + 1) * BLK)
            lh[b, at], ll[b, at] = split(mm3_t(split(get(r, b)), w))
        for c in range(b + 1, nb):
            below, at = slice(c * BLK, nb * BLK), slice(c * BLK, (c + 1) * BLK)
            v = mm3_t((lh[b, below], ll[b, below]), (lh[b, at], ll[b, at]))
            for r in range(c, nb):
                idx = block(r, c)
                full[idx] = full[idx] - v[(r - c) * BLK:(r - c + 1) * BLK].reshape(4, 4, 8, BLK)
        meanwhile(b)

def extend(b, ext, lh, ll, wh, wl):
    at, rest = slice(b * BLK, (b + 1) * BLK), slice((b + 1) * BLK, ext.shape[1])
    y = mm3_t(split(ext[:, at]), (wh[b], wl[b]))
    ext[:, at] = y
    if rest.start < rest.stop:
        ext[:, rest] = ext[:, rest] - mm3_t(split(y), (lh[b, rest], ll[b, rest]))

def whole(lengths, samples, sketch, scale):
    dma = pltpu.SemaphoreType.DMA
    rows, feats = samples.shape
    width = sketch.shape[1]
    chunk = rows // 4
    nb = width // BLK
    return pl.pallas_call(
        functools.partial(whole_kernel, scale),
        out_shape=jax.ShapeDtypeStruct((width // TOKS, feats), F32),
        in_specs=[pl.BlockSpec(memory_space=pltpu.VMEM), pl.BlockSpec(memory_space=pl.ANY), pl.BlockSpec(memory_space=pl.ANY)],
        out_specs=pl.BlockSpec(memory_space=pltpu.VMEM),
        scratch_shapes=[pltpu.VMEM((2, 4, chunk, feats), BF16), pltpu.VMEM(sketch.shape, BF16), pltpu.VMEM((2, chunk, 128), F32),
                        pltpu.VMEM((2 * chunk, width), BF16), pltpu.VMEM((2 * chunk, width), BF16),
                        reduce_scratch(G_STREAMS, (4,)), reduce_scratch(C_STREAMS, ()), pltpu.VMEM((2, 4, 4, 4, 8, 640), F32),
                        pltpu.VMEM((16, width), F32), pltpu.VMEM((nb, width, BLK), BF16), pltpu.VMEM((nb, width, BLK), BF16),
                        pltpu.VMEM((nb, BLK, BLK), BF16), pltpu.VMEM((nb, BLK, BLK), BF16),
                        pltpu.VMEM((2, 16, 8, BLK), F32), pltpu.VMEM((BLK, feats), F32),
                        dma((3, 3, 3)), dma((3, 3, 3)), dma((3, 4)), dma((3, 4)),
                        dma((SUBS,)), dma((SUBS, 3)), dma((SUBS, 3)), dma((SUBS, 4)), dma((SUBS, 4)), dma((1,)),
                        dma((TOKS,)), dma((TOKS,))],
        compiler_params=pltpu.CompilerParams(collective_id=1, has_side_effects=True, vmem_limit_bytes=60 << 20),
        cost_estimate=pl.CostEstimate(flops=15_000_000_000, bytes_accessed=8 << 20, transcendentals=0),
    )(lengths, samples.reshape(4, chunk, feats), sketch)


def shards(samples, lengths, sketch):
    scale = math.sqrt(sketch.shape[1] / (samples.shape[0] // 2 * lax.axis_size("tok")))
    return whole(lengths, samples, sketch, scale)


def solution(mesh):
    in_specs = (P("tok", "col"), P(), P())
    out_specs = P("tok", "col")
    return jax.shard_map(shards, mesh=mesh, in_specs=in_specs, out_specs=out_specs, check_vma=False)
```

```python
import functools
import math

import jax
import jax.numpy as jnp
from jax import lax
from jax.experimental import pallas as pl
from jax.experimental.pallas import tpu as pltpu
from jax.sharding import PartitionSpec as P

F32, BF16 = jnp.float32, jnp.bfloat16
MESH = pl.DeviceIdType.MESH
G_STREAMS = ((0, 256), (256, 256), (512, 128))
C_STREAMS = ((0, 256), (256, 384), (640, 384))
G_PLACES = ((0, 512), (1, 384), (1, 0), (0, 0))
SUBS = 4
TOKS = 32
BLK = 128

class Place:
    def __init__(self):
        self.tok = lax.axis_index("tok")
        self.core = lax.rem(self.tok, 2)
        self.at = (lax.axis_index("col"), self.tok // 8, lax.rem(self.tok // 2, 4))

    def device(self, at, core):
        z, y, x = at
        return ((y * 4 + x) * 2 + core, z)

    def mate(self):
        return self.device(self.at, 1 - self.core)

    def peer(self, axis, d):
        at = list(self.at)
        at[axis] = lax.rem(at[axis] + d, 4)
        return self.device(at, self.core)

    def step(self, axis, d):
        return lax.rem(self.at[axis] + d + 4, 4)

def remote(src, dst, ssem, rsem, dev):
    return pltpu.make_async_remote_copy(src_ref=src, dst_ref=dst, send_sem=ssem, recv_sem=rsem, device_id=dev, device_id_type=MESH)

def pick(axis, p, lanes):
    idx = [slice(None)] * 3
    idx[axis] = p
    return tuple(idx) + (slice(None), pl.ds(*lanes))

def greet(place):
    barrier = pltpu.get_barrier_semaphore()
    def hello(d, _):
        pl.semaphore_signal(barrier, inc=1, device_id=(lax.rem(place.tok + d, TOKS), place.at[0]), device_id_type=MESH)
        return 0
    lax.fori_loop(1, TOKS, hello, 0)
    for d in range(1, 4):
        pl.semaphore_signal(barrier, inc=1, device_id=place.peer(0, d), device_id_type=MESH)
    pl.semaphore_wait(barrier, TOKS + 2)

class Reduction:
    def __init__(self, place, streams, acc, r1, a1, r2, a2, r3, a3, ps, pr):
        self.place, self.streams = place, streams
        self.acc, self.r, self.a = acc, (r1, r2, r3), (a1, a2, a3)
        self.ps, self.pr = ps, pr
        self.copies = {}

    def order(self, s):
        return (s, (s + 1) % 3, (s + 2) % 3)

    def sub(self, s, phase, p):
        if phase == 0:
            return pick(s, p, self.streams[s])
        if phase == 1 and s == 1:
            return (slice(None), p)
        return (p,)

    def source(self, s, phase):
        return self.acc if phase == 0 else self.a[phase - 1][s]

    def send(self, phase, s):
        axis = self.order(s)[phase]
        for d in (2, 1, 3):
            src = self.source(s, phase).at[self.sub(s, phase, self.place.step(axis, d))]
            c = remote(src, self.r[phase][s].at[d - 1], self.ps.at[phase, s, d - 1], self.pr.at[phase, s, d - 1], self.place.peer(axis, d))
            c.start()
            self.copies[phase, s, d] = c

    def gather(self, phase, s):
        axis = self.order(s)[phase]
        total = self.source(s, phase)[self.sub(s, phase, self.place.step(axis, 0))]
        for d in range(1, 4):
            self.copies[phase, s, d].wait_recv()
        r = self.r[phase][s]
        self.a[phase][s][...] = (total + r[0]) + (r[1] + r[2])

    def share(self, s):
        axis = self.order(s)[2]
        for d in (2, 1, 3):
            c = remote(self.a[1][s], self.r[2][s].at[d - 1], self.ps.at[2, s, d - 1], self.pr.at[2, s, d - 1], self.place.peer(axis, d))
            c.start()
            self.copies[2, s, d] = c

    def shared(self, s):
        for d in range(1, 4):
            self.copies[2, s, d].wait_recv()
        r = self.r[2][s]
        return (self.a[1][s][...] + r[0]) + (r[1] + r[2])

    def finish(self):
        for c in self.copies.values():
            c.wait_send()

class Spread:
    def __init__(self, red, full, ss, rs, fs, fr):
        self.red, self.full, self.place = red, full, red.place
        self.ss, self.rs, self.fs, self.fr = ss, rs, fs, fr
        self.sends = []

    def region(self, s, fixed, core):
        idx = [slice(None)] * 3
        for axis, p in fixed.items():
            idx[axis] = p
        return self.full.at[(core,) + tuple(idx) + (slice(None), pl.ds(*self.red.streams[s]))]

    def seed(self, s):
        idx = [slice(None)] * 3
        for axis in self.red.order(s)[:2]:
            idx[axis] = self.place.at[axis]
        o, n = self.red.streams[s]
        self.full[(self.place.core,) + tuple(idx) + (slice(None), slice(o, o + n))] = self.red.shared(s)

    def fixed(self, s, phase, d):
        axes = self.red.order(s)[:3 - phase]
        f = {a: self.place.at[a] for a in axes}
        f[axes[-1]] = self.place.step(axes[-1], -d)
        return f, axes[-1]

    def copy(self, phase, s, d, held):
        f, axis = self.fixed(s, phase, held)
        reg = self.region(s, f, self.place.core)
        return remote(reg, reg, self.ss.at[phase, s, d - 1], self.rs.at[phase, s, d - 1], self.place.peer(axis, d))

    def send(self, phase, s):
        for d in (2, 1, 3):
            c = self.copy(phase, s, d, 0)
            c.start()
            self.sends.append(c)

    def arrived(self, phase, s, d):
        self.copy(phase, s, d, d).wait_recv()

    def wait(self, phase, s):
        for d in range(1, 4):
            self.arrived(phase, s, d)

    def passing(self, s, d, core):
        f, _ = self.fixed(s, 2, d)
        reg = self.region(s, f, core)
        return remote(reg, reg, self.fs.at[s, d], self.fr.at[s, d], self.place.mate())

    def forward(self, s, d):
        c = self.passing(s, d, self.place.core)
        c.start()
        self.sends.append(c)

    def finish(self, s):
        for d in (0, 1, 3, 2):
            self.passing(s, d, 1 - self.place.core).wait_recv()

    def sent(self):
        for c in self.sends:
            c.wait_send()

class Rows:
    def __init__(self, place, x, held, loc, zs, zr, ms, mr):
        self.place, self.x, self.held = place, x, held
        self.loc, self.zs, self.zr, self.ms, self.mr = loc, zs, zr, ms, mr
        self.step = held.shape[2] // SUBS

    def rows(self, sub):
        return pl.ds(sub * self.step, self.step)

    def slot(self, core, d, sub):
        return self.held.at[core, self.place.step(0, -d), self.rows(sub)]

    def own(self, sub):
        return pltpu.make_async_copy(self.x.at[self.place.at[0], self.rows(sub)], self.slot(self.place.core, 0, sub), self.loc.at[sub])

    def across(self, d, sub):
        return remote(self.x.at[self.place.step(0, d), self.rows(sub)], self.slot(self.place.core, 0, sub),
                      self.zs.at[sub, d - 1], self.zr.at[sub, d - 1], self.place.peer(0, d))

    def passing(self, d, sub, core):
        src = self.x.at[self.place.at[0], self.rows(sub)] if d == 0 else self.slot(core, d, sub)
        return remote(src, self.slot(core, d, sub), self.ms.at[sub, d], self.mr.at[sub, d], self.place.mate())

    def take(self, sub):
        self.own(sub).wait()
        for d in (1, 3, 2):
            remote(self.slot(self.place.core, d, sub), self.slot(self.place.core, d, sub),
                   self.zs.at[sub, d - 1], self.zr.at[sub, d - 1], self.place.peer(0, d)).wait_recv()
            self.passing(d, sub, self.place.core).start()

    def take_other(self, sub):
        for d in range(4):
            self.passing(d, sub, 1 - self.place.core).wait_recv()

    def finish(self):
        for sub in range(SUBS):
            for d in range(4):
                self.passing(d, sub, self.place.core).wait_send()
                if d:
                    self.across(d, sub).wait_send()

def over_rows(a, b):
    return lax.dot_general(a, b, (((0,), (0,)), ((), ())), preferred_element_type=F32)

def weights_into(place, lengths, wcol):
    rows = wcol.shape[1]
    assert rows == 1024
    pos = place.at[0] * rows + lax.broadcasted_iota(jnp.int32, (8, 128), 0) * 128 + lax.broadcasted_iota(jnp.int32, (8, 128), 1)
    for k in range(2):
        own = lengths[pl.ds(place.tok - place.core + k, 1), :]
        start = jnp.zeros((8, 128), jnp.int32)
        w = jnp.zeros((8, 128), F32)
        for s in range(lengths.shape[1]):
            count = jnp.broadcast_to(own[:, s:s + 1], (8, 128))
            per = lax.rsqrt(1.0 + 4.0 * count.astype(F32) / float(2 * rows))
            w = w + jnp.where((pos >= start) & (pos < start + count), per, 0.0)
            start = start + count
        wt = w.T
        for a in range(8):
            wcol[k, 128 * a:128 * (a + 1)] = jnp.broadcast_to(wt[:, a:a + 1], (128, 128))

def whole_kernel(scale, len_ref, x_ref, sk_ref, o_ref, held, omega, wcol, sh, sl, gs, cs, full, ext, lh, ll, wh, wl, got, flat, ss, rs, fs, fr, loc, zs, zr, ms, mr, osem, ys, yr):
    place = Place()
    core = place.core
    rows = Rows(place, x_ref, held, loc, zs, zr, ms, mr)
    g = Reduction(place, G_STREAMS, *gs)
    c = Reduction(place, C_STREAMS, *cs)
    sketch = pltpu.make_async_copy(sk_ref, omega, osem.at[0])
    sketch.start()
    for sub in range(SUBS):
        rows.own(sub).start()
    greet(place)
    for sub in range(SUBS):
        for d in (2, 1, 3):
            rows.across(d, sub).start()
        rows.passing(0, sub, core).start()
    weights_into(place, len_ref, wcol)
    g.acc[...] = jnp.zeros_like(g.acc)
    c.acc[...] = jnp.zeros_like(c.acc)
    sketch.wait()
    step = rows.step

    def project(sub, k, which):
        x = jnp.concatenate([held[which, z, pl.ds(sub * step, step)] for z in range(4)], 1)
        prod = jnp.dot(x, omega[...], preferred_element_type=F32)
        w = wcol[which, pl.ds(sub * step, step)]
        s = prod * jnp.concatenate([w] * (omega.shape[1] // 128), 1)
        hi = s.astype(BF16)
        at = pl.ds((2 * sub + k) * step, step)
        sh[at] = hi
        sl[at] = (s - hi.astype(F32)).astype(BF16)

    def chunk(sub, _):
        rows.take(sub)
        project(sub, 0, core)
        rows.take_other(sub)
        project(sub, 1, 1 - core)
        at = pl.ds(2 * sub * step, 2 * step)
        for i in range(4):
            width = 128 * (i + 1)
            far = pl.ds(pl.multiple_of(core * width, 128), width)
            lh, ll, rh, rl = sh[at, 256 * i:256 * (i + 1)], sl[at, 256 * i:256 * (i + 1)], sh[at, far], sl[at, far]
            v = over_rows(lh, rh) + over_rows(lh, rl) + over_rows(ll, rh)
            half, lane = G_PLACES[i]
            g.acc[2 * half:2 * half + 2, :, :, :, lane:lane + width] += v.reshape(2, 4, 4, 8, width)
        return 0

    lax.fori_loop(0, SUBS, chunk, 0)
    for s in range(3):
        g.send(0, s)

    def cross(sub, _):
        mine = pl.ds(pl.multiple_of(core * 128, 128), 128)
        x = jnp.concatenate([
            jnp.concatenate([held[which, z, pl.ds(sub * step, step), mine] for z in range(4)], 1) for which in (core, 1 - core)], 0)
        at = pl.ds(2 * sub * step, 2 * step)
        v = over_rows(x, sh[at]) + over_rows(x, sl[at])
        c.acc[...] += v.reshape(4, 4, 4, 8, omega.shape[1])
        return 0

    lax.fori_loop(0, SUBS, cross, 0)
    sp = Spread(g, full, ss, rs, fs, fr)
    for s in range(3):
        g.gather(0, s)
        g.send(1, s)
    for s in range(3):
        g.gather(1, s)
        g.share(s)
    for s in range(3):
        sp.seed(s)
        sp.send(1, s)
    for s in range(3):
        sp.wait(1, s)
        sp.send(2, s)
        sp.forward(s, 0)
    for d in (1, 3, 2):
        for s in (2, 0, 1):
            sp.arrived(2, s, d)
            sp.forward(s, d)
    for s in range(3):
        c.send(0, s)
    sp.finish(2)

    def settled():
        sp.finish(0)
        sp.finish(1)
        sp.sent()

    result = Result(place, ext, got, flat, ys, yr)

    def meanwhile(b):
        if b == 3:
            for s in range(3):
                c.gather(0, s)
                c.send(1, s)
        if b == 4:
            for s in range(3):
                c.gather(1, s)
                c.send(2, s)
        if b == 6:
            for s in range(3):
                c.gather(2, s)
                o, n = C_STREAMS[s]
                ext[0:8, o:o + n] = c.a[2][s][...]
            ext[8:16, :] = jnp.zeros((8, omega.shape[1]), F32)
        if b >= 6:
            for k in range(0 if b == 6 else b, b + 1):
                extend(k, ext, lh, ll, wh, wl)
                result.send(k)

    factor(full, lh, ll, wh, wl, settled, meanwhile)
    result.finish(o_ref, scale)
    rows.finish()
    g.finish()
    c.finish()

def reduce_scratch(streams, last):
    lanes = sum(n for _, n in streams)
    def per(shape):
        return [pltpu.VMEM(shape + (8, n), F32) for _, n in streams]
    dma = pltpu.SemaphoreType.DMA
    return [pltpu.VMEM((4, 4, 4, 8, lanes), F32), per((3, 4, 4)), per((4, 4)), per((3, 4)), per((4,)), per((3,) + last), per(last),
            dma((3, 3, 3)), dma((3, 3, 3))]

class Result:
    def __init__(self, place, ext, got, flat, ys, yr):
        self.place, self.ext, self.got, self.flat, self.ys, self.yr = place, ext, got, flat, ys, yr

    def copy(self, to, owner, b):
        return remote(self.ext.at[0:8, BLK * b:BLK * (b + 1)], self.got.at[lax.rem(owner, 2), owner // 2], self.ys.at[to], self.yr.at[owner], (to, self.place.at[0]))

    def send(self, b):
        tok = self.place.tok
        for to in range(4 * b, 4 * b + 4):
            @pl.when(tok != to)
            def _():
                self.copy(to, tok, b).start()
        @pl.when(tok // 4 == b)
        def _():
            self.got[self.place.core, tok // 2] = self.ext[0:8, BLK * b:BLK * (b + 1)]

    def finish(self, o_ref, scale):
        tok = self.place.tok
        def landed(d, _):
            src = lax.rem(tok + d, TOKS)
            self.copy(src, src, 0).wait_recv()
            return 0
        lax.fori_loop(1, TOKS, landed, 0)
        for k in range(2):
            self.flat[:, 128 * k:128 * (k + 1)] = self.got[k].reshape(128, 128).T * scale
        o_ref[...] = self.flat[pl.ds(pl.multiple_of(lax.rem(tok, 4) * 32, 32), 32)]
        def sent(d, _):
            self.copy(lax.rem(tok + d, TOKS), tok, 0).wait_send()
            return 0
        lax.fori_loop(1, TOKS, sent, 0)

def split(x):
    hi = x.astype(BF16)
    return hi, (x - hi.astype(F32)).astype(BF16)

def mm_t(a, b):
    return lax.dot_general(a, b, (((1,), (1,)), ((), ())), preferred_element_type=F32)

def mm3_t(a, b):
    (ah, al), (bh, bl) = a, b
    return mm_t(ah, bh) + (mm_t(ah, bl) + mm_t(al, bh))

def inverse_factor(m):
    n = m.shape[0]
    nb = n // 8
    sub = lax.broadcasted_iota(jnp.int32, (8, n), 0)
    lane = lax.broadcasted_iota(jnp.int32, (8, n), 1)
    row = lambda v, i: jnp.broadcast_to(v[i:i + 1], (8, n))
    col = lambda v, i: jnp.broadcast_to(v[:, i:i + 1], (8, n))
    z = [m[8 * q:8 * q + 8] for q in range(nb)]
    diag = [col(z[0], k) for k in range(8)]
    out = []
    for s in range(nb):
        at = 8 * s
        inside = (lane >= at) & (lane < at + 8)
        zs = jnp.where(inside, jnp.where(lane == at + sub, 1.0, 0.0), z[s])
        more = s + 1 < nb
        if more:
            below = [col(z[s + 1], at + k) for k in range(8)]
            ahead = [col(z[s + 1], at + 8 + k) for k in range(8)]
        l = [[None] * 8 for _ in range(8)]
        r, x, c = [], [], []
        w = None
        for k in range(8):
            r.append(lax.rsqrt(row(diag[k], k)))
            dk = diag[k] * r[k]
            for j in range(k + 1, 8):
                l[j][k] = row(diag[k], j) * r[k]
                diag[j] = diag[j] - dk * l[j][k]
            if more:
                ck = below[k]
                for j in range(k):
                    ck = ck - c[j] * l[k][j]
                c.append(ck * r[k])
                for j in range(8):
                    ahead[j] = ahead[j] - c[k] * row(c[k], j)
            xk = row(zs, k)
            for j in range(k):
                xk = xk - l[k][j] * x[j]
            x.append(xk * r[k])
            w = x[k] if w is None else jnp.where(sub == k, x[k], w)
        out.append(jnp.where(lane < at + 8, w, 0.0))
        if more:
            diag = ahead
            zq = jnp.where(inside, 0.0, z[s + 1])
            for k in range(8):
                zq = zq - c[k] * x[k]
            z[s + 1] = zq
        if s + 2 < nb:
            y = [None] * 8
            for k in range(7, -1, -1):
                yk = x[k]
                for i in range(7, k, -1):
                    yk = yk - l[i][k] * y[i]
                y[k] = yk * r[k]
            for q in range(s + 2, nb):
                zq = jnp.where(inside, 0.0, z[q])
                for k in range(7, -1, -1):
                    zq = zq - col(z[q], at + k) * y[k]
                z[q] = zq
    return jnp.concatenate(out, 0)
def block(r, c):
    i = r // 2
    width = 128 * (i + 1)
    core = (128 * c) // width
    half, lane = G_PLACES[i]
    lane += 128 * c - core * width
    return (core, 2 * half + r % 2, slice(None), slice(None), slice(None), slice(lane, lane + BLK))

def factor(full, lh, ll, wh, wl, settled, meanwhile):
    nb = wh.shape[0]
    get = lambda r, c: full[block(r, c)].reshape(BLK, BLK)
    for b in range(nb):
        w = split(inverse_factor(get(b, b)))
        wh[b], wl[b] = w
        if b == 0:
            settled()
        for r in range(b + 1, nb):
            at = slice(r * BLK, (r + 1) * BLK)
            lh[b, at], ll[b, at] = split(mm3_t(split(get(r, b)), w))
        for c in range(b + 1, nb):
            below, at = slice(c * BLK, nb * BLK), slice(c * BLK, (c + 1) * BLK)
            v = mm3_t((lh[b, below], ll[b, below]), (lh[b, at], ll[b, at]))
            for r in range(c, nb):
                idx = block(r, c)
                full[idx] = full[idx] - v[(r - c) * BLK:(r - c + 1) * BLK].reshape(4, 4, 8, BLK)
        meanwhile(b)

def extend(b, ext, lh, ll, wh, wl):
    at, rest = slice(b * BLK, (b + 1) * BLK), slice((b + 1) * BLK, ext.shape[1])
    y = mm3_t(split(ext[:, at]), (wh[b], wl[b]))
    ext[:, at] = y
    if rest.start < rest.stop:
        ext[:, rest] = ext[:, rest] - mm3_t(split(y), (lh[b, rest], ll[b, rest]))

def whole(lengths, samples, sketch, scale):
    dma = pltpu.SemaphoreType.DMA
    rows, feats = samples.shape
    width = sketch.shape[1]
    chunk = rows // 4
    nb = width // BLK
    return pl.pallas_call(
        functools.partial(whole_kernel, scale),
        out_shape=jax.ShapeDtypeStruct((width // TOKS, feats), F32),
        in_specs=[pl.BlockSpec(memory_space=pltpu.VMEM), pl.BlockSpec(memory_space=pl.ANY), pl.BlockSpec(memory_space=pl.ANY)],
        out_specs=pl.BlockSpec(memory_space=pltpu.VMEM),
        scratch_shapes=[pltpu.VMEM((2, 4, chunk, feats), BF16), pltpu.VMEM(sketch.shape, BF16), pltpu.VMEM((2, chunk, 128), F32),
                        pltpu.VMEM((2 * chunk, width), BF16), pltpu.VMEM((2 * chunk, width), BF16),
                        reduce_scratch(G_STREAMS, (4,)), reduce_scratch(C_STREAMS, ()), pltpu.VMEM((2, 4, 4, 4, 8, 640), F32),
                        pltpu.VMEM((16, width), F32), pltpu.VMEM((nb, width, BLK), BF16), pltpu.VMEM((nb, width, BLK), BF16),
                        pltpu.VMEM((nb, BLK, BLK), BF16), pltpu.VMEM((nb, BLK, BLK), BF16),
                        pltpu.VMEM((2, 16, 8, BLK), F32), pltpu.VMEM((BLK, feats), F32),
                        dma((3, 3, 3)), dma((3, 3, 3)), dma((3, 4)), dma((3, 4)),
                        dma((SUBS,)), dma((SUBS, 3)), dma((SUBS, 3)), dma((SUBS, 4)), dma((SUBS, 4)), dma((1,)),
                        dma((TOKS,)), dma((TOKS,))],
        compiler_params=pltpu.CompilerParams(collective_id=1, has_side_effects=True, vmem_limit_bytes=60 << 20),
        cost_estimate=pl.CostEstimate(flops=15_000_000_000, bytes_accessed=8 << 20, transcendentals=0),
    )(lengths, samples.reshape(4, chunk, feats), sketch)


def shards(samples, lengths, sketch):
    scale = math.sqrt(sketch.shape[1] / (samples.shape[0] // 2 * lax.axis_size("tok")))
    return whole(lengths, samples, sketch, scale)


def solution(mesh):
    in_specs = (P("tok", "col"), P(), P())
    out_specs = P("tok", "col")
    return jax.shard_map(shards, mesh=mesh, in_specs=in_specs, out_specs=out_specs, check_vma=False)
```
